128 devices in a mesh: turn: 8 (over x, core), river: 16 (over z, y).
Axes of the slice: x: 4, y: 4, z: 4, core: 2. Of those that a mesh axis runs over, the one named last changes fastest.
Arguments:
- river_regret: float32 [9216, 256], P(('turn', 'river')), may hold values from -8 to 8
- turn_regret: float32 [1024, 128], P(('turn', 'river')), may hold values from -8 to 8
- river_bucket: int32 [24, 32, 1081], P('turn', 'river'), may hold values from 0 to 9215
- turn_bucket: int32 [24, 1081], P('turn'), may hold values from 0 to 1023
- ranks: int32 [24, 32, 1081], P('turn', 'river'), may hold values from 0 to 7461
- turn_card: int32 [24], P('turn'), may hold values from 0 to 46, as said below
- river_card: int32 [24, 32], P('turn', 'river'), may hold values from 0 to 46, as said below
- player_range: float32 [64, 1081], replicated, may hold values from 0.1 to 1
- opp_range: float32 [64, 1081], replicated, may hold values from 0.1 to 1
- call_prob: bfloat16 [24, 32, 128, 1081], P('turn', 'river'), may hold values from 0 to 1
- base_pot: float32 [64], replicated, may hold values from 2 to 24
Outputs:
- new_river_regret: float32 [9216, 256], P(('turn', 'river'))
- new_turn_regret: float32 [1024, 128], P(('turn', 'river'))
- br_value: float32 [24, 64, 1081], P('turn', 'river')
The draws below stay inside these ranges and needn't reach their ends.
Inputs may be any that keep to these rules, and one draw needn't show every extreme that they name: `turn_card`: turn cards are distinct cards of 0 to 46. `river_card`: the river cards of one turn are distinct and differ from that turn's card.
All inputs are finite; a program needn't handle non-finite values.
Results may differ from the reference program's by a relative error of at most 0.0003.
Values sent between devices are 32-bit elements; how exact they have to be, the bound alone decides.
No kernel may reach another device: no remote copies, remote signals or barrier semaphores. Data moves between devices by JAX's collectives and lax.ppermute only.
A program may use at most 128 MiB of HBM per device.

```python
import math
import jax
import jax.numpy as jnp
import numpy as np
from jax import lax

CARDS = 47
H = 1081
RB = 9216
TB = 1024
G = 64
TURNS = 24
RIVERS = 32


def shared_turns(key):
    return jax.random.permutation(key, CARDS)[:TURNS].astype(jnp.int32)


def draw_turn_card(key, part):
    return shared_turns(key)


def draw_river_card(key, part):
    turns = shared_turns(key)
    key = jax.random.fold_in(key, 5)
    keys = jax.random.split(key, TURNS)

    def one_turn(turn_key, turn_value):
        picked = jax.random.permutation(turn_key, CARDS - 1)[:RIVERS].astype(jnp.int32)
        return picked + (picked >= turn_value).astype(jnp.int32)
    return jax.vmap(one_turn)(keys, turns).astype(jnp.int32)


def draw_river_bucket(key, part):
    key = jax.random.fold_in(key, 11)
    picked = jax.random.randint(key, (TURNS, RIVERS, H), 0, RB, dtype=jnp.int32)
    picked = picked.at[:, 0, 0].set(RB - 1).at[:, 0, 1].set(0)
    return picked.astype(jnp.int32)


def plant(result, rng, low, largest):
    index_at = [jax.random.randint(jax.random.fold_in(rng, axis), (), 0, length) for axis, length in enumerate(result.shape)]
    main_axis = result.shape.index(max(result.shape))
    neighbour = index_at[:main_axis] + [(index_at[main_axis] + 1) % result.shape[main_axis]] + index_at[main_axis + 1:]
    return result.at[tuple(index_at)].set(low).at[tuple(neighbour)].set(largest)


def level_of(own_key, extent, pieces, smallest, top_value):
    def one(axis_at, parts):
        draws = jax.random.uniform(jax.random.fold_in(jax.random.fold_in(own_key, 6), axis_at), (parts,), jnp.float32, smallest / len(pieces), top_value / len(pieces))
        return jnp.repeat(jnp.exp(draws), extent[axis_at] // parts).reshape((-1,) + (1,) * (len(extent) - axis_at - 1))

    gain = one(*pieces[0])
    for cut in pieces[1:]:
        gain = gain * one(*cut)
    return gain


def centred(rng, shape, width, bound, cuts=(), kind=jnp.bfloat16):
    level = level_of(rng, shape, cuts, -0.22, 0.18) if cuts else 1.0
    values = jax.random.normal(rng, shape, jnp.float32) * width * level
    return jnp.minimum(jnp.maximum(values, -bound), bound).astype(kind)


def setup_inputs(seed: int = 0) -> dict:
    streams_of = jax.random.split(jax.random.key(seed), 12)
    river_regret = centred(streams_of[0], (RB, 4 * G), 2.0, 8.0, ((0, 128),), jnp.float32)
    turn_regret = centred(streams_of[1], (TB, 2 * G), 2.0, 8.0, ((0, 128),), jnp.float32)
    river_bucket = draw_river_bucket(jax.random.fold_in(streams_of[11], 71), 0)
    turn_bucket = plant(jax.random.randint(streams_of[3], (TURNS, H), 0, TB), jax.random.fold_in(streams_of[3], 1), 0, TB - 1).astype(jnp.int32)
    ranks = plant(jax.random.randint(streams_of[4], (TURNS, RIVERS, H), 0, 7462), jax.random.fold_in(streams_of[4], 1), 0, 7461).astype(jnp.int32)
    turn_card = draw_turn_card(jax.random.fold_in(streams_of[11], 71), 0)
    river_card = draw_river_card(jax.random.fold_in(streams_of[11], 71), 0)
    player_range = jnp.clip(jnp.exp(jax.random.uniform(streams_of[7], (G, H), jnp.float32, math.log(0.1), math.log(1.0))), 0.1, 1.0)
    opp_range = jnp.clip(jnp.exp(jax.random.uniform(streams_of[8], (G, H), jnp.float32, math.log(0.1), math.log(1.0))), 0.1, 1.0)
    call_prob = jnp.clip(1.0 * jax.random.uniform(streams_of[9], (TURNS, RIVERS, 2 * G, H), jnp.float32) ** level_of(streams_of[9], (TURNS, RIVERS, 2 * G, H), ((0, 8), (1, 16)), -0.2, 0.2), 0.0, 1.0).astype(jnp.bfloat16)
    base_pot = jnp.clip(jnp.exp(jax.random.uniform(streams_of[10], (G,), jnp.float32, math.log(2.0), math.log(24.0))), 2.0, 24.0)
    return dict(river_regret=river_regret, turn_regret=turn_regret, river_bucket=river_bucket, turn_bucket=turn_bucket, ranks=ranks, turn_card=turn_card, river_card=river_card, player_range=player_range, opp_range=opp_range, call_prob=call_prob, base_pot=base_pot)


def matching(regret):
    positive = jnp.maximum(regret, 0.0)
    weight_sum = jnp.sum(positive, axis=-1, keepdims=True)
    safe_sum = jnp.where(weight_sum > 0.0, weight_sum, 1.0)
    return jnp.where(weight_sum > 0.0, positive / safe_sum, 0.5)


def board_payoffs(hand_first, hand_second, rank_row, turn_value, river_value):
    playable = (hand_first != turn_value) & (hand_second != turn_value) & (hand_first != river_value) & (hand_second != river_value)
    disjoint = ((hand_first[:, None] != hand_first[None, :]) & (hand_first[:, None] != hand_second[None, :])
                & (hand_second[:, None] != hand_first[None, :]) & (hand_second[:, None] != hand_second[None, :]))
    usable = disjoint & playable[:, None] & playable[None, :]
    direct = jnp.where(usable, 1.0, 0.0).astype(jnp.float32)
    rank_sign = jnp.sign((rank_row[:, None] - rank_row[None, :]).astype(jnp.float32))
    return (direct * rank_sign).astype(jnp.bfloat16), direct.astype(jnp.bfloat16)


def board_values(signed, direct, regret_rows, turn_strat, mine_reach, theirs, called, stakes, folding):
    hand_count, columns = regret_rows.shape
    group_count = columns // 4
    river_strat = matching(regret_rows.reshape(hand_count, group_count, 2, 2))
    player_reach = (mine_reach[:, :, None, None] * turn_strat[:, :, :, None] * river_strat).astype(jnp.bfloat16)
    call_share = called.T.astype(jnp.float32).reshape(hand_count, group_count, 2)
    show_reach = jnp.stack([jnp.broadcast_to(theirs[:, :, None], (hand_count, group_count, 2)),
                            theirs[:, :, None] * call_share], axis=-1).astype(jnp.bfloat16)
    fold_reach = (theirs[:, :, None] * (1.0 - call_share)).astype(jnp.bfloat16)
    show_sums = jnp.dot(signed.astype(jnp.float32),
                        jnp.concatenate([show_reach.reshape(hand_count, columns), player_reach.reshape(hand_count, columns)], axis=1).astype(jnp.float32),
                        preferred_element_type=jnp.float32)
    fold_sums = jnp.dot(direct.astype(jnp.float32),
                        jnp.concatenate([fold_reach.reshape(hand_count, 2 * group_count), player_reach[:, :, :, 1].reshape(hand_count, 2 * group_count)], axis=1).astype(jnp.float32),
                        preferred_element_type=jnp.float32)
    showdown = show_sums[:, :columns].reshape(hand_count, group_count, 2, 2)
    against = show_sums[:, columns:].reshape(hand_count, group_count, 2, 2)
    fold_total = fold_sums[:, :2 * group_count].reshape(hand_count, group_count, 2)
    against_bet = fold_sums[:, 2 * group_count:].reshape(hand_count, group_count, 2)
    fold_gain = jnp.stack([jnp.zeros_like(fold_total), folding * fold_total], axis=-1)
    payoff = (stakes * showdown + fold_gain) / hand_count
    node_value = jnp.sum(river_strat * payoff, axis=-1)
    root_value = jnp.sum(turn_strat * node_value, axis=-1)
    river_inc = (payoff - node_value[..., None]).reshape(hand_count, columns)
    turn_inc = (node_value - root_value[..., None]).reshape(hand_count, 2 * group_count)
    check_value = stakes[..., 0] * against[..., 0]
    call_value = stakes[..., 1] * against[..., 1]
    fold_value = -folding * against_bet
    reply = jnp.sum(check_value + jnp.maximum(call_value, fold_value), axis=-1) / hand_count
    return river_inc, turn_inc, reply.T


def reference(river_regret, turn_regret, river_bucket, turn_bucket, ranks, turn_card, river_card, player_range, opp_range, call_prob, base_pot):
    first_np, second_np = np.triu_indices(CARDS, 1)
    hand_first = jnp.asarray(first_np.astype(np.int32))
    hand_second = jnp.asarray(second_np.astype(np.int32))
    mine_reach = player_range.T
    theirs = opp_range.T
    halves = 0.5 * base_pot
    stakes = halves[:, None, None] + jnp.array([[0.0, 2.0], [2.0, 4.0]], jnp.float32)
    folding = halves[:, None] + jnp.array([0.0, 2.0], jnp.float32)
    turn_strat = matching(turn_regret[turn_bucket.reshape(-1)].reshape(TURNS, H, G, 2))

    def turn_step(carry, turn_items):
        river_acc, turn_acc = carry
        strat, turn_value, bucket_rows, rank_rows, river_values, called_rows, turn_ids = turn_items

        def river_step(inner, river_items):
            river_sum, turn_sum, reply_sum = inner
            bucket_row, rank_row, river_value, called = river_items
            signed, direct = board_payoffs(hand_first, hand_second, rank_row, turn_value, river_value)
            river_inc, turn_inc, reply = board_values(signed, direct, river_regret[bucket_row], strat,
                                                      mine_reach, theirs, called, stakes, folding)
            river_sum = river_sum + jax.ops.segment_sum(river_inc, bucket_row, num_segments=RB)
            return (river_sum, turn_sum + turn_inc, reply_sum + reply), None

        start = (river_acc, jnp.zeros((H, 2 * G), jnp.float32), jnp.zeros((G, H), jnp.float32))
        (river_acc, turn_sum, reply_sum), _ = lax.scan(river_step, start, (bucket_rows, rank_rows, river_values, called_rows))
        turn_acc = turn_acc + jax.ops.segment_sum(turn_sum, turn_ids, num_segments=TB)
        return (river_acc, turn_acc), reply_sum / RIVERS

    start = (jnp.zeros((RB, 4 * G), jnp.float32), jnp.zeros((TB, 2 * G), jnp.float32))
    (river_acc, turn_acc), br_value = lax.scan(turn_step, start, (turn_strat, turn_card, river_bucket, ranks, river_card, call_prob, turn_bucket))
    new_river_regret = jnp.maximum(river_regret + river_acc / RIVERS, 0.0)
    new_turn_regret = jnp.maximum(turn_regret + turn_acc / RIVERS, 0.0)
    return new_river_regret, new_turn_regret, br_value
```

```python
import functools

import jax
import jax.numpy as jnp
import ml_dtypes
import numpy as np
from jax import lax
from jax.experimental import pallas as pl
from jax.experimental.pallas import tpu as pltpu
from jax.sharding import Mesh
from jax.sharding import PartitionSpec as P

CARDS = 47
H = CARDS * (CARDS - 1) // 2
HP = 1152
G = 64
C = 2 * G
BF = jnp.bfloat16
F32 = jnp.float32
NT = (((1,), (1,)), ((), ()))
NN = (((1,), (0,)), ((), ()))
TABLES = 4
VMEM_LIMIT = 60 * 1024 * 1024


def constants():
    first, second = np.triu_indices(CARDS, 1)
    share = (
        (first[:, None] == first[None, :])
        | (first[:, None] == second[None, :])
        | (second[:, None] == first[None, :])
        | (second[:, None] == second[None, :])
    )
    disjoint = np.zeros((HP, HP), np.float32)
    disjoint[:H, :H] = ~share
    rows = np.full((8, HP), -1, np.int32)
    rows[0, :H] = first
    rows[1, :H] = second
    cols = np.full((2, HP, 128), -1, np.int32)
    cols[0, :H] = first[:, None]
    cols[1, :H] = second[:, None]
    river_perm = np.zeros((4 * G, 4 * G), np.float32)
    turn_perm = np.zeros((2 * G, 2 * G), np.float32)
    for g in range(G):
        for a in range(2):
            turn_perm[g * 2 + a, a * G + g] = 1
            for b in range(2):
                river_perm[g * 4 + a * 2 + b, b * C + a * G + g] = 1
    return (
        disjoint.astype(ml_dtypes.bfloat16),
        rows,
        cols,
        river_perm.astype(ml_dtypes.bfloat16),
        turn_perm.astype(ml_dtypes.bfloat16),
    )


def parts(x, count):
    out = []
    for _ in range(count):
        piece = x.astype(BF)
        out.append(piece)
        x = x - piece.astype(F32)
    return out


def permuted(x, perm, dims):
    hi, mid, lo = [
        lax.dot_general(piece, perm, dims, preferred_element_type=F32) for piece in parts(x, 3)
    ]
    return (hi + mid) + lo


def first_share(pos0, pos1):
    total = pos0 + pos1
    some = total > 0.0
    safe = jnp.where(some, total, 1.0)
    return jnp.where(some, pos0 / safe, 0.5), jnp.where(some, pos1 / safe, 0.5)


def river_shares(permuted_regret):
    pos = jnp.maximum(permuted_regret, 0.0)
    return first_share(pos[:, :C], pos[:, C:])


def turn_shares(permuted_regret):
    pos = jnp.maximum(permuted_regret, 0.0)
    return first_share(pos, pltpu.roll(pos, G, 1))


def strategy_kernel(river_ref, turn_ref, rperm_ref, tperm_ref, out_ref):
    owned = river_ref.shape[0]
    share, _ = river_shares(permuted(river_ref[...], rperm_ref[...], NN))
    out_ref[:owned, :] = share
    tshare, _ = turn_shares(permuted(turn_ref[...], tperm_ref[...], NN))
    out_ref[owned:, :] = tshare


def update_kernel(
    scale, river_ref, turn_ref, rsum_ref, tsum_ref, rperm_ref, tperm_ref, river_out, turn_out
):
    rp = permuted(river_ref[...], rperm_ref[...], NN)
    s0, s1 = river_shares(rp)
    gain = rsum_ref[...] * scale
    new = jnp.maximum(rp + jnp.concatenate([s1 * gain, -(s0 * gain)], axis=1), 0.0)
    river_out[...] = permuted(new, rperm_ref[...], NT)
    tp = permuted(turn_ref[...], tperm_ref[...], NN)
    _, other = turn_shares(tp)
    new = jnp.maximum(tp + other * (tsum_ref[...] * scale), 0.0)
    turn_out[...] = permuted(new, tperm_ref[...], NT)


def stake_rows(pot_ref):
    pot = pot_ref[...]
    lane = lax.broadcasted_iota(jnp.int32, (1, C), 1)
    bet = 0.5 * jnp.concatenate([pot, pot], axis=1) + jnp.where(lane >= G, 2.0, 0.0)
    return bet * (1.0 / H), (bet + 2.0) * (1.0 / H)


def playable(first, second, turn_value, river_value):
    return (
        (first != turn_value)
        & (second != turn_value)
        & (first != river_value)
        & (second != river_value)
    )


def payoff_kernel(
    rivers,
    bucket_ref,
    tcard_ref,
    rcard_ref,
    rank_ref,
    call_ref,
    opp_ref,
    pot_ref,
    disjoint_ref,
    rows_ref,
    cols_ref,
    signed_ref,
    delta_ref,
    bet_ref,
    table_ref,
    rank_s,
    call_s,
    opp_s,
    show_s,
    fold_s,
    *extra,
):
    board = pl.program_id(0)
    t, r = board // rivers, board % rivers
    tables = (table_ref,) + extra

    @pl.when(board == 0)
    def _():
        rank_s[...] = jnp.zeros_like(rank_s)
        call_s[...] = jnp.zeros_like(call_s)
        opp_s[...] = jnp.zeros_like(opp_s)
        opp_s[:, :H] = opp_ref[...]
        for table in tables:
            table[...] = jnp.zeros_like(table)

    turn_value, river_value = tcard_ref[t], rcard_ref[t, r]
    row_ok = playable(rows_ref[0:1, :], rows_ref[1:2, :], turn_value, river_value)
    col_ok = playable(cols_ref[0], cols_ref[1], turn_value, river_value)

    rank_s[0:1, :H] = rank_ref[0, pl.ds(r, 1), :]
    rank_row = rank_s[0:1, :].astype(F32)
    rank_col = jnp.transpose(jnp.broadcast_to(rank_row, (128, HP)))
    for j in range(HP // 128):
        lanes = slice(j * 128, (j + 1) * 128)
        sign = jnp.clip(rank_col - rank_row[:, lanes], -1.0, 1.0)
        signed_ref[0, :, lanes] = sign.astype(BF) * disjoint_ref[:, lanes]

    theirs = jnp.where(row_ok, opp_s[...], 0.0)
    for j in range(HP // 128):
        lanes = slice(j * 128, (j + 1) * 128)
        width = min(128, H - j * 128)
        call_s[j, :, :width] = call_ref[0, :, j * 128 : j * 128 + width].astype(F32)
        theirs_j = theirs[:, lanes]
        for a in range(2):
            called = call_s[j, pl.ds(a, G, stride=2), :]
            rows = slice(a * G, (a + 1) * G)
            show_s[rows, lanes] = theirs_j.astype(BF)
            show_s[C + a * G : C + (a + 1) * G, lanes] = (theirs_j * called).astype(BF)
            fold_s[rows, lanes] = (theirs_j * (1.0 - called)).astype(BF)

    show = lax.dot_general(signed_ref[0], show_s[...], NT, preferred_element_type=F32)
    fold = lax.dot_general(disjoint_ref[...], fold_s[...], NT, preferred_element_type=F32)
    low, high = stake_rows(pot_ref)
    bet = high * show[:, C:] + low * fold
    bet_ref[0] = jnp.where(col_ok, bet, 0.0)
    delta_ref[0] = jnp.where(col_ok, low * show[:, :C] - bet, 0.0)

    def add_row(h, table):
        k = bucket_ref[t, r, h]
        table[pl.ds(k, 1), :] += delta_ref[0, pl.ds(h, 1), :]

    step = 4 * TABLES

    def add_rows(i, _):
        for j in range(step):
            add_row(i * step + j, tables[j % TABLES])
        return 0

    lax.fori_loop(0, H // step, add_rows, 0)
    for h in range(H // step * step, H):
        add_row(h, tables[h % TABLES])

    @pl.when(board == pl.num_programs(0) - 1)
    def _():
        total = table_ref[...]
        for table in extra:
            total = total + table[...]
        table_ref[...] = total


def reply_kernel(
    rivers,
    river_total,
    bucket_ref,
    tbucket_ref,
    tcard_ref,
    rcard_ref,
    table_ref,
    trow_ref,
    signed_ref,
    delta_ref,
    bet_ref,
    mine_ref,
    pot_ref,
    disjoint_ref,
    cols_ref,
    br_ref,
    gain_ref,
    mine_s,
    turn_s,
    river_s,
    reach_s,
    reply_s,
    node_s,
    trow_s,
    wide_s,
):
    board = pl.program_id(0)
    t, r = board // rivers, board % rivers

    @pl.when(board == 0)
    def _():
        wide_s[...] = jnp.zeros_like(wide_s)
        wide_s[:G, :H] = mine_ref[...]
        wide_s[G:, :H] = mine_ref[...]
        mine_s[...] = jnp.transpose(wide_s[...])
        reply_s[...] = jnp.zeros_like(reply_s)
        node_s[...] = jnp.zeros_like(node_s)
        turn_s[...] = jnp.zeros_like(turn_s)
        river_s[...] = jnp.zeros_like(river_s)
        trow_s[...] = jnp.full_like(trow_s, -1)
        gain_ref[...] = jnp.zeros_like(gain_ref)

    step = 16

    def gather(dst, index):
        def rows(i, _):
            for j in range(step):
                h = i * step + j
                dst[pl.ds(h, 1), :] = table_ref[pl.ds(index(h), 1), :]
            return 0

        lax.fori_loop(0, H // step, rows, 0)
        for h in range(H // step * step, H):
            dst[pl.ds(h, 1), :] = table_ref[pl.ds(index(h), 1), :]

    @pl.when(r == 0)
    def _():
        gather(turn_s, lambda h: tbucket_ref[t, h])

    gather(river_s, lambda h: bucket_ref[t, r, h])

    turn_value, river_value = tcard_ref[t], rcard_ref[t, r]
    col_ok = playable(cols_ref[0], cols_ref[1], turn_value, river_value)
    first = river_s[...]
    reach = jnp.where(col_ok, mine_s[...] * turn_s[...], 0.0)
    reach_s[:, :C] = (reach * first).astype(BF)
    reach_s[:, C:] = (reach * (1.0 - first)).astype(BF)
    against = lax.dot_general(signed_ref[0], reach_s[...], NN, preferred_element_type=F32)
    against_bet = lax.dot_general(
        disjoint_ref[...], reach_s[:, C:], NN, preferred_element_type=F32
    )
    low, high = stake_rows(pot_ref)
    reply = low * against[:, :C] + jnp.maximum(high * against[:, C:], -(low * against_bet))
    reply = jnp.where(col_ok, reply, 0.0)
    node = bet_ref[0] + first * delta_ref[0]

    reply_s[...] = jnp.where(r == 0, reply, reply_s[...] + reply)
    node_s[...] = jnp.where(r == 0, node, node_s[...] + node)

    @pl.when(r == rivers - 1)
    def _():
        flat = jnp.transpose(reply_s[...])
        br_ref[0] = ((flat[:G] + flat[G:]) * (1.0 / river_total))[:, :H]
        nodes = node_s[...]
        diff = nodes - pltpu.roll(nodes, G, 1)
        hi, lo = parts(diff, 2)
        trow_s[0:1, :H] = trow_ref[pl.ds(t, 1), :]
        ids = lax.broadcasted_iota(jnp.int32, (gain_ref.shape[0], HP), 0)
        hot = jnp.where(ids == trow_s[0:1, :], 1.0, 0.0).astype(BF)
        gain_ref[...] += lax.dot_general(hot, hi, NN, preferred_element_type=F32) + lax.dot_general(
            hot, lo, NN, preferred_element_type=F32
        )


def per_device(
    river_regret,
    turn_regret,
    river_bucket,
    turn_bucket,
    ranks,
    turn_card,
    river_card,
    player_range,
    opp_range,
    call_prob,
    base_pot,
):
    turns, rivers, _ = river_bucket.shape
    boards = turns * rivers
    devices = lax.axis_size(("turn", "river"))
    river_total = rivers * lax.axis_size("river")
    owned, towned = river_regret.shape[0], turn_regret.shape[0]
    buckets, tbuckets = owned * devices, towned * devices
    disjoint, rows, cols, rperm, tperm = constants()
    params = pltpu.CompilerParams(vmem_limit_bytes=VMEM_LIMIT)
    pot = base_pot.reshape(1, G)
    calls = call_prob.reshape(boards, C, H)
    rest = owned + towned

    with jax.named_scope("strategies"):
        strategies = pl.pallas_call(
            strategy_kernel,
            out_shape=jax.ShapeDtypeStruct((rest, C), F32),
            compiler_params=params,
            name="strategies",
        )(river_regret, turn_regret, rperm, tperm)
        table = lax.all_gather(strategies, ("turn", "river"), axis=0, tiled=True)

    def whole(shape):
        return pl.BlockSpec(shape, lambda i, *_: (0,) * len(shape))

    def per_board(shape):
        return pl.BlockSpec((1,) + shape, lambda i, *_: (i,) + (0,) * len(shape))

    def per_turn(shape):
        return pl.BlockSpec((1,) + shape, lambda i, *_: (i // rivers,) + (0,) * len(shape))

    with jax.named_scope("payoffs"):
        signed, delta, bet, sums = pl.pallas_call(
            functools.partial(payoff_kernel, rivers),
            grid_spec=pltpu.PrefetchScalarGridSpec(
                num_scalar_prefetch=3,
                grid=(boards,),
                in_specs=[
                    per_turn((rivers, H)),
                    per_board((C, H)),
                    whole((G, H)),
                    whole((1, G)),
                    whole((HP, HP)),
                    whole((8, HP)),
                    whole((2, HP, 128)),
                ],
                out_specs=[
                    per_board((HP, HP)),
                    per_board((HP, C)),
                    per_board((HP, C)),
                    whole((buckets, C)),
                ],
                scratch_shapes=[
                    pltpu.VMEM((8, HP), jnp.int32),
                    pltpu.VMEM((HP // 128, C, 128), F32),
                    pltpu.VMEM((G, HP), F32),
                    pltpu.VMEM((2 * C, HP), BF),
                    pltpu.VMEM((C, HP), BF),
                ]
                + [pltpu.VMEM((buckets, C), F32)] * (TABLES - 1),
            ),
            out_shape=[
                jax.ShapeDtypeStruct((boards, HP, HP), BF),
                jax.ShapeDtypeStruct((boards, HP, C), F32),
                jax.ShapeDtypeStruct((boards, HP, C), F32),
                jax.ShapeDtypeStruct((buckets, C), F32),
            ],
            compiler_params=params,
            name="payoffs",
        )(
            river_bucket,
            turn_card,
            river_card,
            ranks,
            calls,
            opp_range,
            pot,
            disjoint,
            rows,
            cols,
        )

    with jax.named_scope("river_sums"):
        river_sums = lax.psum_scatter(sums, ("turn", "river"), scatter_dimension=0, tiled=True)

    river_at = river_bucket // owned * rest + river_bucket % owned
    turn_at = turn_bucket // towned * rest + owned + turn_bucket % towned
    with jax.named_scope("replies"):
        replies, gains = pl.pallas_call(
            functools.partial(reply_kernel, rivers, river_total),
            grid_spec=pltpu.PrefetchScalarGridSpec(
                num_scalar_prefetch=4,
                grid=(boards,),
                in_specs=[
                    whole((rest * devices, C)),
                    whole((turns, H)),
                    per_board((HP, HP)),
                    per_board((HP, C)),
                    per_board((HP, C)),
                    whole((G, H)),
                    whole((1, G)),
                    whole((HP, HP)),
                    whole((2, HP, 128)),
                ],
                out_specs=[
                    per_turn((G, H)),
                    whole((tbuckets, C)),
                ],
                scratch_shapes=[
                    pltpu.VMEM((HP, C), F32),
                    pltpu.VMEM((HP, C), F32),
                    pltpu.VMEM((HP, C), F32),
                    pltpu.VMEM((HP, 2 * C), BF),
                    pltpu.VMEM((HP, C), F32),
                    pltpu.VMEM((HP, C), F32),
                    pltpu.VMEM((8, HP), jnp.int32),
                    pltpu.VMEM((C, HP), F32),
                ],
            ),
            out_shape=[
                jax.ShapeDtypeStruct((turns, G, H), F32),
                jax.ShapeDtypeStruct((tbuckets, C), F32),
            ],
            compiler_params=params,
            name="replies",
        )(
            river_at,
            turn_at,
            turn_card,
            river_card,
            table,
            turn_bucket,
            signed,
            delta,
            bet,
            player_range,
            pot,
            disjoint,
            cols,
        )

    with jax.named_scope("br_value"):
        br_value = lax.psum_scatter(replies, "river", scatter_dimension=1, tiled=True)
    with jax.named_scope("turn_sums"):
        turn_sums = lax.psum_scatter(gains, ("turn", "river"), scatter_dimension=0, tiled=True)

    with jax.named_scope("update"):
        new_river, new_turn = pl.pallas_call(
            functools.partial(update_kernel, 1.0 / river_total),
            out_shape=[
                jax.ShapeDtypeStruct(river_regret.shape, F32),
                jax.ShapeDtypeStruct(turn_regret.shape, F32),
            ],
            compiler_params=params,
            name="update",
        )(river_regret, turn_regret, river_sums, turn_sums, rperm, tperm)
    return new_river, new_turn, br_value


def solution(mesh):
    both = ("turn", "river")
    placed = (
        P(both, None),
        P(both, None),
        P("turn", "river", None),
        P("turn", None),
        P("turn", "river", None),
        P("turn"),
        P("turn", "river"),
        P(),
        P(),
        P("turn", "river", None, None),
        P(),
    )
    return jax.shard_map(
        per_device,
        mesh=mesh,
        in_specs=placed,
        out_specs=(P(both, None), P(both, None), P("turn", "river", None)),
        check_vma=False,
    )
```

```python
import functools

import jax
import jax.numpy as jnp
import ml_dtypes
import numpy as np
from jax import lax
from jax.experimental import pallas as pl
from jax.experimental.pallas import tpu as pltpu
from jax.sharding import Mesh
from jax.sharding import PartitionSpec as P

CARDS = 47
H = CARDS * (CARDS - 1) // 2
HP = 1152
G = 64
C = 2 * G
BF = jnp.bfloat16
F32 = jnp.float32
NT = (((1,), (1,)), ((), ()))
NN = (((1,), (0,)), ((), ()))
TABLES = 6
UNROLL = 47
INDEX_ROW = 2048
AXES = ("x", "core", "z", "y")
VMEM_LIMIT = 60 * 1024 * 1024


def constants():
    first, second = np.triu_indices(CARDS, 1)
    share = (
        (first[:, None] == first[None, :])
        | (first[:, None] == second[None, :])
        | (second[:, None] == first[None, :])
        | (second[:, None] == second[None, :])
    )
    disjoint = np.zeros((HP, HP), np.float32)
    disjoint[:H, :H] = ~share
    cols = np.full((2, HP, 128), -1, np.int32)
    cols[0, :H] = first[:, None]
    cols[1, :H] = second[:, None]
    holds = np.zeros((64, HP), np.float32)
    holds[first, np.arange(H)] = 1
    holds[second, np.arange(H)] = 1
    holds[CARDS, :H] = 1
    spread_out = np.zeros((HP, 64), np.float32)
    spread_out[:H, :CARDS] = -holds[:CARDS, :H].T
    spread_out[:H, CARDS] = 1
    spread_out = np.concatenate([spread_out] * 3 + [np.zeros_like(spread_out)], axis=1)
    river_perm = np.zeros((4 * G, 4 * G), np.float32)
    turn_perm = np.zeros((2 * G, 2 * G), np.float32)
    for g in range(G):
        for a in range(2):
            turn_perm[g * 2 + a, a * G + g] = 1
            for b in range(2):
                river_perm[g * 4 + a * 2 + b, b * C + a * G + g] = 1
    halves = [m.astype(ml_dtypes.bfloat16) for m in (disjoint, holds, spread_out, river_perm, turn_perm)]
    return halves + [cols]


def others(x, holds_ref, out_of_ref):
    sums = lax.dot_general(holds_ref[...], x, NN, preferred_element_type=F32)
    pieces = parts(sums, 3)
    pieces = jnp.concatenate(pieces + [jnp.zeros_like(pieces[0])], axis=0)
    return x.astype(F32) + lax.dot_general(
        out_of_ref[...], pieces, NN, preferred_element_type=F32
    )


def parts(x, count):
    out = []
    for _ in range(count):
        piece = x.astype(BF)
        out.append(piece)
        x = x - piece.astype(F32)
    return out


def permuted(x, perm, dims):
    hi, mid, lo = [
        lax.dot_general(piece, perm, dims, preferred_element_type=F32) for piece in parts(x, 3)
    ]
    return (hi + mid) + lo


def first_share(pos0, pos1):
    total = pos0 + pos1
    some = total > 0.0
    safe = jnp.where(some, total, 1.0)
    return jnp.where(some, pos0 / safe, 0.5), jnp.where(some, pos1 / safe, 0.5)


def river_shares(permuted_regret):
    pos = jnp.maximum(permuted_regret, 0.0)
    return first_share(pos[:, :C], pos[:, C:])


def turn_shares(permuted_regret):
    pos = jnp.maximum(permuted_regret, 0.0)
    return first_share(pos, pltpu.roll(pos, G, 1))


def strategy_kernel(
    place_ref,
    river_ref,
    turn_ref,
    rperm_ref,
    tperm_ref,
    bucket_ref,
    tbucket_ref,
    out_ref,
    index_ref,
    at_ref,
    tat_ref,
):
    owned, towned = river_ref.shape[0], turn_ref.shape[0]
    rest = owned + towned
    share, _ = river_shares(permuted(river_ref[...], rperm_ref[...], NN))
    out_ref[:owned, :] = share
    tshare, _ = turn_shares(permuted(turn_ref[...], tperm_ref[...], NN))
    out_ref[owned:, :] = tshare

    turns, rivers, _ = bucket_ref.shape
    index_ref[...] = jnp.zeros_like(index_ref)
    tat_ref[...] = jnp.zeros_like(tat_ref)
    for j in range(HP // 128):
        width = min(128, H - j * 128)
        lanes = slice(j * 128, j * 128 + width)
        for t in range(turns):
            tat_ref[t, j : j + 1, :width] = tbucket_ref[t : t + 1, lanes]
            for r in range(rivers):
                index_ref[t * rivers + r, j : j + 1, :width] = bucket_ref[t, r : r + 1, lanes]

    x, core, z, y = (place_ref[i] for i in range(4))

    def placed(bucket, count, offset):
        owner = ((bucket.astype(F32) + 0.5) * (1.0 / count)).astype(jnp.int32)
        row = bucket - owner * count
        down_y = (y - owner) & 3
        down_z = (z - (owner >> 2)) & 3
        other = (core - (owner >> 4)) & 1
        down_x = (x - (owner >> 5)) & 3
        slot = ((other * 4 + down_x) * 4 + down_z) * 4 + down_y
        return slot * rest + offset + row

    at_ref[...] = placed(index_ref[...], owned, 0)
    tat_ref[...] = placed(tat_ref[...], towned, owned)


def update_kernel(
    scale, each, came_ref, river_ref, turn_ref, rperm_ref, tperm_ref, river_out, turn_out, br_out
):
    turns = br_out.shape[0]
    blocks = HP // 128
    came = came_ref[0]
    for source in range(1, came_ref.shape[0]):
        came = came + came_ref[source]
    for t in range(turns):
        for j in range(blocks):
            row = (t * blocks + j) * each
            width = min(128, H - j * 128)
            br_out[t, :, j * 128 : j * 128 + width] = came[row : row + each, :width]
    at = turns * blocks * each
    rsum = came[at + 4 : at + 4 + river_ref.shape[0]]
    tsum = came[at : at + 4]
    rp = permuted(river_ref[...], rperm_ref[...], NN)
    s0, s1 = river_shares(rp)
    gain = rsum * scale
    new = jnp.maximum(rp + jnp.concatenate([s1 * gain, -(s0 * gain)], axis=1), 0.0)
    river_out[...] = permuted(new, rperm_ref[...], NT)
    tp = permuted(turn_ref[...], tperm_ref[...], NN)
    _, other = turn_shares(tp)
    lane = lax.broadcasted_iota(jnp.int32, tsum.shape, 1)
    swapped = pltpu.roll(tsum, G, 1)
    low = jnp.where(lane < G, tsum, -swapped)
    high = jnp.where(lane < G, swapped, -tsum)
    gain = jnp.concatenate([low, high], axis=0) * scale
    turn_out[...] = permuted(jnp.maximum(tp + other * gain, 0.0), tperm_ref[...], NT)


def stake_rows(pot_ref):
    pot = pot_ref[...]
    lane = lax.broadcasted_iota(jnp.int32, (1, C), 1)
    bet = 0.5 * jnp.concatenate([pot, pot], axis=1) + jnp.where(lane >= G, 2.0, 0.0)
    return bet * (1.0 / H), (bet + 2.0) * (1.0 / H)


def playable(first, second, turn_value, river_value):
    return (
        (first != turn_value)
        & (second != turn_value)
        & (first != river_value)
        & (second != river_value)
    )


def for_each_hand(index_ref, board, body):
    base = board * INDEX_ROW

    def some(i, _):
        for j in range(UNROLL):
            h = i * UNROLL + j
            body(h, index_ref[base + h], j)
        return 0

    lax.fori_loop(0, H // UNROLL, some, 0)


def widen(wide_s, narrow_ref, out_s):
    wide_s[...] = jnp.zeros_like(wide_s)
    wide_s[:G, :H] = narrow_ref[...]
    wide_s[G:, :H] = narrow_ref[...]
    out_s[...] = jnp.transpose(wide_s[...])


def payoff_kernel(
    rivers,
    tcard_ref,
    rcard_ref,
    rank_ref,
    call_ref,
    opp_ref,
    pot_ref,
    disjoint_ref,
    holds_ref,
    out_of_ref,
    tperm_ref,
    cols_ref,
    signed_ref,
    delta_ref,
    bet_ref,
    rank_s,
    call_s,
    wide_s,
    opp_s,
    show_s,
):
    board = pl.program_id(0)
    t, r = board // rivers, board % rivers

    @pl.when(board == 0)
    def _():
        rank_s[...] = jnp.zeros_like(rank_s)
        call_s[rivers * H :, :] = jnp.zeros((rivers * (HP - H), C), F32)
        widen(wide_s, opp_ref, opp_s)

    @pl.when(r == 0)
    def _():
        called = call_ref[0].reshape(rivers * H, C)
        call_s[: rivers * H, :] = lax.dot_general(
            called, tperm_ref[...], NN, preferred_element_type=F32
        )

    col_ok = playable(cols_ref[0], cols_ref[1], tcard_ref[t], rcard_ref[r, t])
    rank_s[0:1, :H] = rank_ref[0, pl.ds(r, 1), :]
    rank_row = rank_s[0:1, :].astype(F32)
    rank_col = jnp.transpose(jnp.broadcast_to(rank_row, (128, HP)))
    for j in range(HP // 128):
        lanes = slice(j * 128, (j + 1) * 128)
        sign = jnp.clip(rank_col - rank_row[:, lanes], -1.0, 1.0)
        signed_ref[0, :, lanes] = sign.astype(BF) * disjoint_ref[:, lanes]

    called = call_s[pl.ds(r, HP, stride=rivers), :]
    theirs = jnp.where(col_ok, opp_s[...], 0.0)
    show_s[:, :C] = theirs.astype(BF)
    show_s[:, C:] = (theirs * called).astype(BF)
    show = lax.dot_general(signed_ref[0], show_s[...], NN, preferred_element_type=F32)
    fold = others((theirs * (1.0 - called)).astype(BF), holds_ref, out_of_ref)
    low, high = stake_rows(pot_ref)
    bet = high * show[:, C:] + low * fold
    bet_ref[0] = jnp.where(col_ok, bet, 0.0)
    delta_ref[0] = jnp.where(col_ok, low * show[:, :C] - bet, 0.0)


def sum_kernel(index_ref, place_ref, delta_ref, mine_ref, theirs_ref, *tables):
    board = pl.program_id(0)

    @pl.when(board == 0)
    def _():
        for table in tables:
            table[...] = jnp.zeros_like(table)

    def add_row(h, k, j):
        table = tables[j % TABLES]
        table[pl.ds(k, 1), :] += delta_ref[0, pl.ds(h, 1), :]

    for_each_hand(index_ref, board, add_row)

    @pl.when(board == pl.num_programs(0) - 1)
    def _():
        x, core = place_ref[0], place_ref[1]
        half = mine_ref.shape[1] // 2
        order = ((2, 0), (1, 1), (2, 1), (3, 0), (1, 0), (3, 1), (0, 0), (0, 1))
        for i, (s, part) in enumerate(order):
            for out_ref, c in ((mine_ref, core), (theirs_ref, 1 - core)):
                at = pl.multiple_of((((x + s) & 3) * 4 + c * 2 + part) * half, 8)
                total = tables[0][pl.ds(at, half), :]
                for table in tables[1:]:
                    total = total + table[pl.ds(at, half), :]
                out_ref[i // 2, i % 2 * half : (i % 2 + 1) * half, :] = total


def node_kernel(
    rivers,
    pieces,
    bucket_ref,
    tbucket_ref,
    trow_ref,
    delta_ref,
    bet_ref,
    *refs,
):
    piece_refs, (first_ref, strat_ref, gain_ref, table_s, node_s, trow_s, sem) = (
        refs[:pieces],
        refs[pieces:],
    )
    board = pl.program_id(0)
    t, r = board // rivers, board % rivers

    @pl.when(board == 0)
    def _():
        at, copies = 0, []
        for i, piece in enumerate(piece_refs):
            rows = piece.shape[0]
            copies.append(pltpu.make_async_copy(piece, table_s.at[pl.ds(at, rows)], sem.at[i]))
            copies[-1].start()
            at += rows
        node_s[...] = jnp.zeros_like(node_s)
        trow_s[...] = jnp.full_like(trow_s, -1)
        gain_ref[...] = jnp.zeros_like(gain_ref)
        for copy in copies:
            copy.wait()

    def gather(dst, index, at):
        dst[0, H:, :] = jnp.zeros((HP - H, C), F32)

        def take(h, k, j):
            dst[0, pl.ds(h, 1), :] = table_s[pl.ds(k, 1), :]

        for_each_hand(index, at, take)

    @pl.when(r == 0)
    def _():
        gather(strat_ref, tbucket_ref, t)

    gather(first_ref, bucket_ref, board)
    node = bet_ref[0] + first_ref[0] * delta_ref[0]
    node_s[...] = jnp.where(r == 0, node, node_s[...] + node)

    @pl.when(r == rivers - 1)
    def _():
        nodes = node_s[...]
        hi, lo = parts(nodes - pltpu.roll(nodes, G, 1), 2)
        both = jnp.concatenate([hi[:, :G], lo[:, :G]], axis=1)
        trow_s[0:1, :H] = trow_ref[pl.ds(t, 1), :]
        trow = trow_s[0:1, :]
        row = lax.broadcasted_iota(jnp.int32, (gain_ref.shape[0], HP), 0)
        bucket = row // 4 * 8 + row % 4

        def sums(ids):
            hot = jnp.where(ids == trow, 1.0, 0.0).astype(BF)
            out = lax.dot_general(hot, both, NN, preferred_element_type=F32)
            return out + pltpu.roll(out, G, 1)

        lane = lax.broadcasted_iota(jnp.int32, gain_ref.shape, 1)
        gain_ref[...] += jnp.where(lane < G, sums(bucket), sums(bucket + 4))


def reply_kernel(
    turns,
    rivers,
    river_total,
    tcard_ref,
    rcard_ref,
    first_ref,
    strat_ref,
    signed_ref,
    mine_ref,
    pot_ref,
    holds_ref,
    out_of_ref,
    cols_ref,
    out_ref,
    mine_s,
    reach_s,
    reply_s,
    wide_s,
):
    board = pl.program_id(0)
    t, r = board // rivers, board % rivers

    @pl.when(board == 0)
    def _():
        widen(wide_s, mine_ref, mine_s)
        reply_s[...] = jnp.zeros_like(reply_s)

    col_ok = playable(cols_ref[0], cols_ref[1], tcard_ref[t], rcard_ref[r, t])
    first = first_ref[0]
    reach = jnp.where(col_ok, mine_s[...] * strat_ref[0], 0.0)
    reach_s[:, :C] = (reach * first).astype(BF)
    reach_s[:, C:] = (reach * (1.0 - first)).astype(BF)
    against = lax.dot_general(signed_ref[0], reach_s[...], NN, preferred_element_type=F32)
    against_bet = others(reach_s[:, C:], holds_ref, out_of_ref)
    low, high = stake_rows(pot_ref)
    reply = low * against[:, :C] + jnp.maximum(high * against[:, C:], -(low * against_bet))
    reply = jnp.where(col_ok, reply, 0.0)
    reply_s[...] = jnp.where(r == 0, reply, reply_s[...] + reply)

    @pl.when(r == rivers - 1)
    def _():
        flat = jnp.transpose(reply_s[...])
        flat = (flat[:G] + flat[G:]) * (1.0 / river_total)
        owners = out_ref.shape[0]
        each = G // owners
        blocks = HP // 128
        for turn in range(turns):

            @pl.when(t == turn)
            def _():
                for j in range(blocks):
                    piece = flat[:, j * 128 : (j + 1) * 128].reshape(owners, each, 128)
                    row = (turn * blocks + j) * each
                    out_ref[:, row : row + each, :] = piece


def shifted(x, axis, shift):
    return lax.ppermute(x, axis, [(i, (i + shift) % 4) for i in range(4)])


def spread(x, axis):
    return jnp.concatenate([x] + [shifted(x, axis, s) for s in (1, 2, 3)], axis=0)


def block(x, at):
    return lax.dynamic_index_in_dim(x, at, 0, keepdims=False)


def per_device(
    river_regret,
    turn_regret,
    river_bucket,
    turn_bucket,
    ranks,
    turn_card,
    river_card,
    player_range,
    opp_range,
    call_prob,
    base_pot,
):
    turns, rivers, _ = river_bucket.shape
    boards = turns * rivers
    devices = 128
    owners = 16
    each = G // owners
    river_total = rivers * owners
    owned, towned = river_regret.shape[0], turn_regret.shape[0]
    buckets, tbuckets = owned * devices, towned * devices
    disjoint, holds, out_of, rperm, tperm, cols = constants()
    params = pltpu.CompilerParams(vmem_limit_bytes=VMEM_LIMIT)
    pot = base_pot.reshape(1, G)
    calls = jnp.transpose(call_prob, (0, 3, 1, 2))
    river_at_turn = river_card.T
    place = jnp.stack([lax.axis_index(a) for a in AXES]).astype(jnp.int32)
    rest = owned + towned
    turn_row = turns * (HP // 128) * each
    river_row = turn_row + towned // 2
    sent_rows = river_row + owned
    vmem, smem = (pl.BlockSpec(memory_space=space) for space in (pltpu.VMEM, pltpu.SMEM))

    with jax.named_scope("strategies"):
        strategies, *indices = pl.pallas_call(
            strategy_kernel,
            in_specs=[smem] + [vmem] * 6,
            out_shape=[
                jax.ShapeDtypeStruct((rest, C), F32),
                jax.ShapeDtypeStruct((boards, INDEX_ROW // 128, 128), jnp.int32),
                jax.ShapeDtypeStruct((boards, INDEX_ROW // 128, 128), jnp.int32),
                jax.ShapeDtypeStruct((turns, INDEX_ROW // 128, 128), jnp.int32),
            ],
            compiler_params=params,
            name="strategies",
        )(place, river_regret, turn_regret, rperm, tperm, river_bucket, turn_bucket)
        index, river_at, turn_at = (a.reshape(-1) for a in indices)
        plane = spread(spread(strategies, "y"), "z")
        far, up, down = (shifted(plane, "x", s) for s in (2, 1, 3))
        calls, _ = lax.optimization_barrier((calls, plane))

    def whole(shape):
        return pl.BlockSpec(shape, lambda i, *_: (0,) * len(shape))

    def per_board(shape):
        return pl.BlockSpec((1,) + shape, lambda i, *_: (i,) + (0,) * len(shape))

    def per_turn(shape):
        return pl.BlockSpec((1,) + shape, lambda i, *_: (i // rivers,) + (0,) * len(shape))

    with jax.named_scope("payoffs"):
        signed, delta, bet = pl.pallas_call(
            functools.partial(payoff_kernel, rivers),
            grid_spec=pltpu.PrefetchScalarGridSpec(
                num_scalar_prefetch=2,
                grid=(boards,),
                in_specs=[
                    per_turn((rivers, H)),
                    per_turn((H, rivers, C)),
                    whole((G, H)),
                    whole((1, G)),
                    whole((HP, HP)),
                    whole((64, HP)),
                    whole((HP, 256)),
                    whole((C, C)),
                    whole((2, HP, 128)),
                ],
                out_specs=[
                    per_board((HP, HP)),
                    per_board((HP, C)),
                    per_board((HP, C)),
                ],
                scratch_shapes=[
                    pltpu.VMEM((8, HP), jnp.int32),
                    pltpu.VMEM((rivers * HP, C), F32),
                    pltpu.VMEM((C, HP), F32),
                    pltpu.VMEM((HP, C), F32),
                    pltpu.VMEM((HP, 2 * C), BF),
                ],
            ),
            out_shape=[
                jax.ShapeDtypeStruct((boards, HP, HP), BF),
                jax.ShapeDtypeStruct((boards, HP, C), F32),
                jax.ShapeDtypeStruct((boards, HP, C), F32),
            ],
            compiler_params=params,
            cost_estimate=pl.CostEstimate(
                flops=22 * 10**9, bytes_accessed=10**6, transcendentals=0
            ),
            name="payoffs",
        )(
            turn_card,
            river_at_turn,
            ranks,
            calls,
            opp_range,
            pot,
            disjoint,
            holds,
            out_of,
            tperm,
            cols,
        )

    with jax.named_scope("river_sums"):
        mine, theirs = pl.pallas_call(
            sum_kernel,
            grid_spec=pltpu.PrefetchScalarGridSpec(
                num_scalar_prefetch=2,
                grid=(boards,),
                in_specs=[per_board((HP, C))],
                out_specs=[whole((4, owners * owned, C))] * 2,
                scratch_shapes=[pltpu.VMEM((buckets, C), F32)] * TABLES,
            ),
            out_shape=[jax.ShapeDtypeStruct((4, owners * owned, C), F32)] * 2,
            compiler_params=params,
            cost_estimate=pl.CostEstimate(
                flops=22 * 10**9, bytes_accessed=10**6, transcendentals=0
            ),
            name="sums",
        )(index, place, delta)
        theirs, up, far, down = lax.optimization_barrier((theirs, up, far, down))
        own = [plane, up, far, down]
        pieces = own + [lax.ppermute(piece, "core", [(0, 1), (1, 0)]) for piece in own]
        got = lax.ppermute(theirs, "core", [(0, 1), (1, 0)])
        up_now, down_now, later, kept = (mine[i] + got[i] for i in range(4))
        from_below, from_above = shifted(up_now, "x", 1), shifted(down_now, "x", 3)
        later, delta = lax.optimization_barrier((later, delta))

    with jax.named_scope("nodes"):
        first, strat, gains = pl.pallas_call(
            functools.partial(node_kernel, rivers, len(pieces)),
            grid_spec=pltpu.PrefetchScalarGridSpec(
                num_scalar_prefetch=2,
                grid=(boards,),
                in_specs=[
                    whole((turns, H)),
                    per_board((HP, C)),
                    per_board((HP, C)),
                ]
                + [pl.BlockSpec(memory_space=pl.ANY)] * len(pieces),
                out_specs=[
                    per_board((HP, C)),
                    per_turn((HP, C)),
                    whole((tbuckets // 2, C)),
                ],
                scratch_shapes=[
                    pltpu.VMEM((rest * devices, C), F32),
                    pltpu.VMEM((HP, C), F32),
                    pltpu.VMEM((8, HP), jnp.int32),
                    pltpu.SemaphoreType.DMA((len(pieces),)),
                ],
            ),
            out_shape=[
                jax.ShapeDtypeStruct((boards, HP, C), F32),
                jax.ShapeDtypeStruct((turns, HP, C), F32),
                jax.ShapeDtypeStruct((tbuckets // 2, C), F32),
            ],
            compiler_params=params,
            cost_estimate=pl.CostEstimate(
                flops=22 * 10**9, bytes_accessed=10**6, transcendentals=0
            ),
            name="nodes",
        )(river_at, turn_at, turn_bucket, delta, bet, *pieces)

    with jax.named_scope("river_sums"):
        gains, from_below, from_above = lax.optimization_barrier((gains, from_below, from_above))
        half = owners * owned // 2
        below = shifted(later[:half] + from_below[:half], "x", 1)
        above = shifted(later[half:] + from_above[:half], "x", 3)

    with jax.named_scope("turn_sums"):
        x, core = place[0], place[1]
        pairs = gains.reshape(4, 2, -1, C)
        held = lax.dynamic_index_in_dim(pairs, core, 1, keepdims=False)
        lent = lax.dynamic_index_in_dim(pairs, 1 - core, 1, keepdims=False)
        held = held + lax.ppermute(lent, "core", [(0, 1), (1, 0)])
        turn_parts = [block(held, x)]
        turn_parts += [shifted(block(held, (x + s) % 4), "x", s) for s in (2, 1, 3)]

    with jax.named_scope("replies"):
        replies = pl.pallas_call(
            functools.partial(reply_kernel, turns, rivers, river_total),
            grid_spec=pltpu.PrefetchScalarGridSpec(
                num_scalar_prefetch=2,
                grid=(boards,),
                in_specs=[
                    per_board((HP, C)),
                    per_turn((HP, C)),
                    per_board((HP, HP)),
                    whole((G, H)),
                    whole((1, G)),
                    whole((64, HP)),
                    whole((HP, 256)),
                    whole((2, HP, 128)),
                ],
                out_specs=whole((owners, sent_rows, 128)),
                scratch_shapes=[
                    pltpu.VMEM((HP, C), F32),
                    pltpu.VMEM((HP, 2 * C), BF),
                    pltpu.VMEM((HP, C), F32),
                    pltpu.VMEM((C, HP), F32),
                ],
            ),
            out_shape=jax.ShapeDtypeStruct((owners, sent_rows, 128), F32),
            compiler_params=params,
            cost_estimate=pl.CostEstimate(
                flops=18 * 10**9, bytes_accessed=10**6, transcendentals=0
            ),
            name="replies",
        )(
            turn_card,
            river_at_turn,
            first,
            strat,
            signed,
            player_range,
            pot,
            holds,
            out_of,
            cols,
        )

    with jax.named_scope("exchange"):
        replies, below, above, turn_parts = lax.optimization_barrier(
            (replies, below, above, turn_parts)
        )
        turn_sums = sum(turn_parts[1:], turn_parts[0])
        column = kept + jnp.concatenate([below + from_above[half:], above + from_below[half:]])
        sent = replies.at[:, turn_row:river_row].set(turn_sums.reshape(owners, -1, 128))
        sent = sent.at[:, river_row:].set(column.reshape(owners, -1, 128))
        came = lax.all_to_all(sent, ("z", "y"), 0, 0)

    with jax.named_scope("update"):
        new_river, new_turn, br_value = pl.pallas_call(
            functools.partial(update_kernel, 1.0 / river_total, each),
            out_shape=[
                jax.ShapeDtypeStruct(river_regret.shape, F32),
                jax.ShapeDtypeStruct(turn_regret.shape, F32),
                jax.ShapeDtypeStruct((turns, each, H), F32),
            ],
            compiler_params=params,
            name="update",
        )(came, river_regret, turn_regret, rperm, tperm)
    return new_river, new_turn, br_value


def solution(mesh):
    mesh = Mesh(mesh.devices.reshape(4, 2, 4, 4), AXES)
    turn, river = AXES[:2], AXES[2:]
    placed = (
        P(AXES, None),
        P(AXES, None),
        P(turn, river, None),
        P(turn, None),
        P(turn, river, None),
        P(turn),
        P(turn, river),
        P(),
        P(),
        P(turn, river, None, None),
        P(),
    )
    return jax.shard_map(
        per_device,
        mesh=mesh,
        in_specs=placed,
        out_specs=(P(AXES, None), P(AXES, None), P(turn, river, None)),
        check_vma=False,
    )
```

```python
import functools

import jax
import jax.numpy as jnp
import ml_dtypes
import numpy as np
from jax import lax
from jax.experimental import pallas as pl
from jax.experimental.pallas import tpu as pltpu
from jax.sharding import Mesh
from jax.sharding import PartitionSpec as P

CARDS = 47
H = CARDS * (CARDS - 1) // 2
HP = 1152
G = 64
C = 2 * G
BF = jnp.bfloat16
F32 = jnp.float32
NT = (((1,), (1,)), ((), ()))
NN = (((1,), (0,)), ((), ()))
TABLES = 6
UNROLL = 47
CHUNKS = 3
INDEX_ROW = 2048
RANKS = 16384.0
AXES = ("x", "core", "z", "y")
VMEM_LIMIT = 60 * 1024 * 1024


def constants():
    first, second = np.triu_indices(CARDS, 1)
    share = (
        (first[:, None] == first[None, :])
        | (first[:, None] == second[None, :])
        | (second[:, None] == first[None, :])
        | (second[:, None] == second[None, :])
    )
    disjoint = np.zeros((HP, HP), np.float32)
    disjoint[:H, :H] = ~share
    cards = np.full((8, HP), -1, np.int32)
    cards[0, :H] = first
    cards[1, :H] = second
    holds = np.zeros((64, HP), np.float32)
    holds[first, np.arange(H)] = 1
    holds[second, np.arange(H)] = 1
    holds[CARDS, :H] = 1
    spread_out = np.zeros((HP, 64), np.float32)
    spread_out[:H, :CARDS] = -holds[:CARDS, :H].T
    spread_out[:H, CARDS] = 1
    spread_out = np.concatenate([spread_out] * 3 + [np.zeros_like(spread_out)], axis=1)
    river_perm = np.zeros((4 * G, 4 * G), np.float32)
    turn_perm = np.zeros((2 * G, 2 * G), np.float32)
    for g in range(G):
        for a in range(2):
            turn_perm[g * 2 + a, a * G + g] = 1
            for b in range(2):
                river_perm[g * 4 + a * 2 + b, b * C + a * G + g] = 1
    halves = [m.astype(ml_dtypes.bfloat16) for m in (disjoint, holds, spread_out, river_perm, turn_perm)]
    return halves + [cards]


def others(x, holds_ref, out_of_ref):
    sums = lax.dot_general(holds_ref[...], x, NN, preferred_element_type=F32)
    pieces = parts(sums, 3)
    pieces = jnp.concatenate(pieces + [jnp.zeros_like(pieces[0])], axis=0)
    return x.astype(F32) + lax.dot_general(
        out_of_ref[...], pieces, NN, preferred_element_type=F32
    )


def parts(x, count):
    out = []
    for _ in range(count):
        piece = x.astype(BF)
        out.append(piece)
        x = x - piece.astype(F32)
    return out


def permuted(x, perm, dims):
    hi, mid, lo = [
        lax.dot_general(piece, perm, dims, preferred_element_type=F32) for piece in parts(x, 3)
    ]
    return (hi + mid) + lo


def first_share(pos0, pos1):
    total = pos0 + pos1
    some = total > 0.0
    safe = jnp.where(some, total, 1.0)
    return jnp.where(some, pos0 / safe, 0.5), jnp.where(some, pos1 / safe, 0.5)


def river_shares(permuted_regret):
    pos = jnp.maximum(permuted_regret, 0.0)
    return first_share(pos[:, :C], pos[:, C:])


def turn_shares(permuted_regret):
    pos = jnp.maximum(permuted_regret, 0.0)
    return first_share(pos, pltpu.roll(pos, G, 1))


def strategy_kernel(
    place_ref,
    river_ref,
    turn_ref,
    rperm_ref,
    tperm_ref,
    bucket_ref,
    tbucket_ref,
    out_ref,
    index_ref,
    at_ref,
    tat_ref,
):
    owned, towned = river_ref.shape[0], turn_ref.shape[0]
    rest = owned + towned
    share, _ = river_shares(permuted(river_ref[...], rperm_ref[...], NN))
    tshare, _ = turn_shares(permuted(turn_ref[...], tperm_ref[...], NN))
    for i in range(out_ref.shape[0]):
        out_ref[i, :owned, :] = share
        out_ref[i, owned:, :] = tshare

    turns, rivers, _ = bucket_ref.shape
    index_ref[...] = jnp.zeros_like(index_ref)
    tat_ref[...] = jnp.zeros_like(tat_ref)
    for j in range(HP // 128):
        width = min(128, H - j * 128)
        lanes = slice(j * 128, j * 128 + width)
        for t in range(turns):
            tat_ref[t, j : j + 1, :width] = tbucket_ref[t : t + 1, lanes]
            for r in range(rivers):
                index_ref[t * rivers + r, j : j + 1, :width] = bucket_ref[t, r : r + 1, lanes]

    x, core = place_ref[0], place_ref[1]

    def placed(bucket, count, offset):
        owner = ((bucket.astype(F32) + 0.5) * (1.0 / count)).astype(jnp.int32)
        row = bucket - owner * count
        other = (core - (owner >> 4)) & 1
        slot = (other * 4 + ((x - (owner >> 5)) & 3)) * 16 + (owner & 15)
        return slot * rest + offset + row

    at_ref[...] = placed(index_ref[...], owned, 0)
    tat_ref[...] = placed(tat_ref[...], towned, owned)


def update_kernel(
    scale, each, came_ref, river_ref, turn_ref, rperm_ref, tperm_ref, river_out, turn_out, br_out
):
    turns = br_out.shape[0]
    blocks = HP // 128
    came = came_ref[0]
    for source in range(1, came_ref.shape[0]):
        came = came + came_ref[source]
    for t in range(turns):
        for j in range(blocks):
            row = (t * blocks + j) * each
            width = min(128, H - j * 128)
            br_out[t, :, j * 128 : j * 128 + width] = came[row : row + each, :width]
    at = turns * blocks * each
    rsum = came[at + 4 : at + 4 + river_ref.shape[0]]
    tsum = came[at : at + 4]
    rp = permuted(river_ref[...], rperm_ref[...], NN)
    s0, s1 = river_shares(rp)
    gain = rsum * scale
    new = jnp.maximum(rp + jnp.concatenate([s1 * gain, -(s0 * gain)], axis=1), 0.0)
    river_out[...] = permuted(new, rperm_ref[...], NT)
    tp = permuted(turn_ref[...], tperm_ref[...], NN)
    _, other = turn_shares(tp)
    lane = lax.broadcasted_iota(jnp.int32, tsum.shape, 1)
    swapped = pltpu.roll(tsum, G, 1)
    low = jnp.where(lane < G, tsum, -swapped)
    high = jnp.where(lane < G, swapped, -tsum)
    gain = jnp.concatenate([low, high], axis=0) * scale
    turn_out[...] = permuted(jnp.maximum(tp + other * gain, 0.0), tperm_ref[...], NT)


def stake_rows(pot_ref):
    pot = pot_ref[...]
    lane = lax.broadcasted_iota(jnp.int32, (1, C), 1)
    bet = 0.5 * jnp.concatenate([pot, pot], axis=1) + jnp.where(lane >= G, 2.0, 0.0)
    return bet * (1.0 / H), (bet + 2.0) * (1.0 / H)


def playable(first, second, turn_value, river_value):
    return (
        (first != turn_value)
        & (second != turn_value)
        & (first != river_value)
        & (second != river_value)
    )


def for_each_hand(index_ref, board, body):
    base = board * INDEX_ROW

    def some(i, _):
        for j in range(UNROLL):
            h = i * UNROLL + j
            body(h, index_ref[base + h], j)
        return 0

    lax.fori_loop(0, H // UNROLL, some, 0)


def widen(wide_s, narrow_ref, out_s):
    wide_s[...] = jnp.zeros_like(wide_s)
    wide_s[:G, :H] = narrow_ref[...]
    wide_s[G:, :H] = narrow_ref[...]
    out_s[...] = jnp.transpose(wide_s[...])


def sign_matrix(rank_ref, r, turn_value, river_value, cards_ref, disjoint_ref, rank_s, signed_s):
    out = jnp.logical_not(
        playable(cards_ref[0:1, :], cards_ref[1:2, :], turn_value, river_value)
    )
    rank_s[r : r + 1, :H] = rank_ref[0, r : r + 1, :]
    rank_row = rank_s[r : r + 1, :].astype(F32) + jnp.where(out, RANKS, 0.0)
    rank_col = jnp.transpose(jnp.broadcast_to(rank_row, (128, HP)))
    for j in range(HP // 128):
        lanes = slice(j * 128, (j + 1) * 128)
        more = (rank_col - rank_row[:, lanes]).astype(BF)
        bound = disjoint_ref[:, lanes]
        signed_s[r, :, lanes] = jnp.maximum(jnp.minimum(more, bound), -bound)
    return rank_col < RANKS


def payoff_kernel(
    rivers,
    start,
    tcard_ref,
    rcard_ref,
    rank_ref,
    call_ref,
    opp_ref,
    pot_ref,
    disjoint_ref,
    holds_ref,
    out_of_ref,
    tperm_ref,
    cards_ref,
    *refs,
):
    (
        delta_ref,
        bet_ref,
        rank_s,
        call_s,
        wide_s,
        opp_s,
        show_s,
        signed_s,
    ) = refs[-8:]
    t = pl.program_id(0) + start

    @pl.when(t == start)
    def _():
        rank_s[...] = jnp.zeros_like(rank_s)
        call_s[rivers * H :, :] = jnp.zeros((rivers * (HP - H), C), F32)
        widen(wide_s, opp_ref, opp_s)

    call_s[: rivers * H, :] = lax.dot_general(
        call_ref[0].reshape(rivers * H, C), tperm_ref[...], NN, preferred_element_type=F32
    )
    low, high = stake_rows(pot_ref)
    bets = 0.0
    for r in range(rivers):
        col_ok = sign_matrix(
            rank_ref, r, tcard_ref[t], rcard_ref[r, t], cards_ref, disjoint_ref, rank_s, signed_s
        )
        called = call_s[pl.ds(r, HP, stride=rivers), :]
        theirs = jnp.where(col_ok, opp_s[...], 0.0)
        show_s[r, :, :C] = theirs.astype(BF)
        show_s[r, :, C:] = (theirs * called).astype(BF)
        show = lax.dot_general(signed_s[r], show_s[r], NN, preferred_element_type=F32)
        fold = others((theirs * (1.0 - called)).astype(BF), holds_ref, out_of_ref)
        bet = jnp.where(col_ok, high * show[:, C:] + low * fold, 0.0)
        delta_ref[r] = jnp.where(col_ok, low * show[:, :C], 0.0) - bet
        bets = bets + bet
    bet_ref[0] = bets


def sum_kernel(index_ref, place_ref, delta_ref, mine_ref, theirs_ref, *tables):
    board = pl.program_id(0)

    @pl.when(board == 0)
    def _():
        for table in tables:
            table[...] = jnp.zeros_like(table)

    def add_row(h, k, j):
        table = tables[j % TABLES]
        table[pl.ds(k, 1), :] += delta_ref[0, pl.ds(h, 1), :]

    for_each_hand(index_ref, board, add_row)

    @pl.when(board == pl.num_programs(0) - 1)
    def _():
        core = place_ref[1]
        rows = mine_ref.shape[1]
        for s in range(mine_ref.shape[0]):
            for out_ref, c in ((mine_ref, core), (theirs_ref, 1 - core)):
                at = pl.multiple_of((s * 2 + c) * rows, 8)
                total = tables[0][pl.ds(at, rows), :]
                for table in tables[1:]:
                    total = total + table[pl.ds(at, rows), :]
                out_ref[s] = total


def reply_kernel(
    turns,
    rivers,
    river_total,
    pieces,
    bucket_ref,
    tbucket_ref,
    tcard_ref,
    rcard_ref,
    rank_ref,
    trow_ref,
    delta_ref,
    bet_ref,
    mine_ref,
    pot_ref,
    disjoint_ref,
    holds_ref,
    out_of_ref,
    cards_ref,
    *refs,
):
    piece_refs = refs[:pieces]
    (
        out_ref,
        gain_ref,
        table_s,
        rows_s,
        mine_s,
        wide_s,
        rank_s,
        trow_s,
        col_s,
        reach_s,
        sums_s,
        reply_s,
        sem,
    ) = refs[pieces:]
    t = pl.program_id(0)
    now, later = t % 2, (t + 1) % 2
    kinds = rivers + 1

    def take_rows(first, count, turn, slot):
        for j in range(count):
            h = first + j
            k = tbucket_ref[turn * INDEX_ROW + h]
            rows_s[slot, 0, pl.ds(h, 1), :] = table_s[pl.ds(k, 1), :]
            for r in range(rivers):
                k = bucket_ref[(turn * rivers + r) * INDEX_ROW + h]
                rows_s[slot, r + 1, pl.ds(h, 1), :] = table_s[pl.ds(k, 1), :]

    @pl.when(t == 0)
    def _():
        at, copies = 0, []
        for i, piece in enumerate(piece_refs):
            rows = piece.shape[0]
            copies.append(pltpu.make_async_copy(piece, table_s.at[pl.ds(at, rows)], sem.at[i]))
            copies[-1].start()
            at += rows
        rank_s[...] = jnp.zeros_like(rank_s)
        trow_s[...] = jnp.full_like(trow_s, -1)
        gain_ref[...] = jnp.zeros_like(gain_ref)
        widen(wide_s, mine_ref, mine_s)
        for slot in range(2):
            for kind in range(kinds):
                rows_s[slot, kind, H:, :] = jnp.zeros((HP - H, C), F32)
        for copy in copies:
            copy.wait()

        def some(i, _):
            take_rows(i * UNROLL, UNROLL, 0, 0)
            return 0

        lax.fori_loop(0, H // UNROLL, some, 0)

    low, high = stake_rows(pot_ref)
    reach = mine_s[...] * rows_s[now, 0]
    nodes = bet_ref[0]
    for r in range(rivers):
        first = rows_s[now, r + 1]
        out = jnp.logical_not(
            playable(cards_ref[0:1, :], cards_ref[1:2, :], tcard_ref[t], rcard_ref[r, t])
        )
        rank_s[r : r + 1, :H] = rank_ref[0, r : r + 1, :]
        rank_row = rank_s[r : r + 1, :].astype(F32) + jnp.where(out, RANKS, 0.0)
        col_s[r] = jnp.transpose(jnp.broadcast_to(rank_row, (128, HP)))
        col_ok = col_s[r] < RANKS
        reach_s[r, :, :C] = jnp.where(col_ok, reach * first, 0.0).astype(BF)
        reach_s[r, :, C:] = jnp.where(col_ok, reach * (1.0 - first), 0.0).astype(BF)
        sums = lax.dot_general(
            holds_ref[...], reach_s[r, :, C:], NN, preferred_element_type=F32
        )
        split = parts(sums, 3)
        sums_s[r] = jnp.concatenate(split + [jnp.zeros_like(split[0])], axis=0)
        nodes = nodes + first * delta_ref[r]
    rank_rows = [
        rank_s[r : r + 1, :].astype(F32)
        + jnp.where(
            playable(cards_ref[0:1, :], cards_ref[1:2, :], tcard_ref[t], rcard_ref[r, t]),
            0.0,
            RANKS,
        )
        for r in range(rivers)
    ]

    def some_replies(at, count):
        rows = pl.ds(at, count)
        total = 0.0
        for r in range(rivers):
            col = col_s[r, rows, :]
            signed = []
            for j in range(HP // 128):
                lanes = slice(j * 128, (j + 1) * 128)
                more = (col - rank_rows[r][:, lanes]).astype(BF)
                bound = disjoint_ref[rows, lanes]
                signed.append(jnp.maximum(jnp.minimum(more, bound), -bound))
            against = lax.dot_general(
                jnp.concatenate(signed, axis=1), reach_s[r], NN, preferred_element_type=F32
            )
            against_bet = reach_s[r, rows, C:].astype(F32) + lax.dot_general(
                out_of_ref[rows, :], sums_s[r], NN, preferred_element_type=F32
            )
            reply = low * against[:, :C] + jnp.maximum(
                high * against[:, C:], -(low * against_bet)
            )
            total = total + jnp.where(col < RANKS, reply, 0.0)
        reply_s[rows, :] = total

    chunk = HP // CHUNKS
    taken = -(-H // CHUNKS)

    def with_rows(i, _):
        take_rows(i * taken, taken, t + 1, later)
        some_replies(pl.multiple_of(i * chunk, 128), chunk)
        return 0

    def without_rows(i, _):
        some_replies(pl.multiple_of(i * chunk, 128), chunk)
        return 0

    @pl.when(t < turns - 1)
    def _():
        lax.fori_loop(0, CHUNKS, with_rows, 0)

    @pl.when(t == turns - 1)
    def _():
        lax.fori_loop(0, CHUNKS, without_rows, 0)

    hi, lo = parts(nodes - pltpu.roll(nodes, G, 1), 2)
    both = jnp.concatenate([hi[:, :G], lo[:, :G]], axis=1)
    trow_s[0:1, :H] = trow_ref[pl.ds(t, 1), :]
    trow = trow_s[0:1, :]
    row = lax.broadcasted_iota(jnp.int32, (gain_ref.shape[0], HP), 0)
    bucket = row // 4 * 8 + row % 4

    def sums_of(ids):
        hot = jnp.where(ids == trow, 1.0, 0.0).astype(BF)
        out = lax.dot_general(hot, both, NN, preferred_element_type=F32)
        return out + pltpu.roll(out, G, 1)

    lane = lax.broadcasted_iota(jnp.int32, gain_ref.shape, 1)
    gain_ref[...] += jnp.where(lane < G, sums_of(bucket), sums_of(bucket + 4))

    flat = jnp.transpose(reply_s[...])
    flat = (flat[:G] + flat[G:]) * (1.0 / river_total)
    owners = out_ref.shape[0]
    each = G // owners
    blocks = HP // 128
    for turn in range(turns):

        @pl.when(t == turn)
        def _():
            for j in range(blocks):
                piece = flat[:, j * 128 : (j + 1) * 128].reshape(owners, each, 128)
                row = (turn * blocks + j) * each
                out_ref[:, row : row + each, :] = piece


def shifted(x, axis, shift):
    return lax.ppermute(x, axis, [(i, (i + shift) % 4) for i in range(4)])


def block(x, at):
    return lax.dynamic_index_in_dim(x, at, 0, keepdims=False)


def per_device(
    river_regret,
    turn_regret,
    river_bucket,
    turn_bucket,
    ranks,
    turn_card,
    river_card,
    player_range,
    opp_range,
    call_prob,
    base_pot,
):
    turns, rivers, _ = river_bucket.shape
    boards = turns * rivers
    devices = 128
    owners = 16
    each = G // owners
    river_total = rivers * owners
    owned, towned = river_regret.shape[0], turn_regret.shape[0]
    buckets, tbuckets = owned * devices, towned * devices
    disjoint, holds, out_of, rperm, tperm, cards = constants()
    params = pltpu.CompilerParams(vmem_limit_bytes=VMEM_LIMIT)
    pot = base_pot.reshape(1, G)
    calls = jnp.transpose(call_prob, (0, 3, 1, 2))
    river_at_turn = river_card.T
    place = jnp.stack([lax.axis_index(a) for a in AXES]).astype(jnp.int32)
    rest = owned + towned
    turn_row = turns * (HP // 128) * each
    river_row = turn_row + towned // 2
    sent_rows = river_row + owned
    vmem, smem = (pl.BlockSpec(memory_space=space) for space in (pltpu.VMEM, pltpu.SMEM))

    with jax.named_scope("strategies"):
        strategies, *indices = pl.pallas_call(
            strategy_kernel,
            in_specs=[smem] + [vmem] * 6,
            out_shape=[
                jax.ShapeDtypeStruct((owners, rest, C), F32),
                jax.ShapeDtypeStruct((boards, INDEX_ROW // 128, 128), jnp.int32),
                jax.ShapeDtypeStruct((boards, INDEX_ROW // 128, 128), jnp.int32),
                jax.ShapeDtypeStruct((turns, INDEX_ROW // 128, 128), jnp.int32),
            ],
            compiler_params=params,
            name="strategies",
        )(place, river_regret, turn_regret, rperm, tperm, river_bucket, turn_bucket)
        index, river_at, turn_at = (a.reshape(-1) for a in indices)
        plane = lax.all_to_all(strategies, ("z", "y"), 0, 0).reshape(-1, C)

    def whole(shape):
        return pl.BlockSpec(shape, lambda i, *_: (0,) * len(shape))

    def per_turn(shape, count=1):
        return pl.BlockSpec((count,) + shape, lambda i, *_: (i,) + (0,) * len(shape))

    def per_board(shape):
        return per_turn(shape, rivers)

    def payoffs(start, count, known=()):
        def of_turn(shape, each_turn=1):
            return pl.BlockSpec(
                (each_turn,) + shape, lambda i, *_: (i + start,) + (0,) * len(shape)
            )

        return pl.pallas_call(
            functools.partial(payoff_kernel, rivers, start),
            grid_spec=pltpu.PrefetchScalarGridSpec(
                num_scalar_prefetch=2,
                grid=(count,),
                in_specs=[
                    of_turn((rivers, H)),
                    of_turn((H, rivers, C)),
                    whole((G, H)),
                    whole((1, G)),
                    whole((HP, HP)),
                    whole((64, HP)),
                    whole((HP, 256)),
                    whole((C, C)),
                    whole((8, HP)),
                ]
                + [pl.BlockSpec(memory_space=pl.ANY)] * len(known),
                out_specs=[of_turn((HP, C), rivers), of_turn((HP, C))],
                scratch_shapes=[
                    pltpu.VMEM((8, HP), jnp.int32),
                    pltpu.VMEM((rivers * HP, C), F32),
                    pltpu.VMEM((C, HP), F32),
                    pltpu.VMEM((HP, C), F32),
                    pltpu.VMEM((rivers, HP, 2 * C), BF),
                    pltpu.VMEM((rivers, HP, HP), BF),
                ],
            ),
            out_shape=[
                jax.ShapeDtypeStruct((boards, HP, C), F32),
                jax.ShapeDtypeStruct((turns, HP, C), F32),
            ],
            input_output_aliases={11 + i: i for i in range(len(known))},
            compiler_params=params,
            cost_estimate=pl.CostEstimate(
                flops=count * 8 * 10**9, bytes_accessed=10**6, transcendentals=0
            ),
            name="payoffs",
        )(
            turn_card,
            river_at_turn,
            ranks,
            calls,
            opp_range,
            pot,
            disjoint,
            holds,
            out_of,
            tperm,
            cards,
            *known,
        )

    with jax.named_scope("payoffs"):
        delta, bet = payoffs(0, 1)
    with jax.named_scope("strategies"):
        plane, delta = lax.optimization_barrier((plane, delta))
        up, down = shifted(plane, "x", 1), shifted(plane, "x", 3)
    with jax.named_scope("payoffs"):
        delta, bet = payoffs(1, turns - 1, (delta, bet))
    with jax.named_scope("strategies"):
        up, down, delta = lax.optimization_barrier((up, down, delta))
        far = shifted(up, "x", 1)

    with jax.named_scope("river_sums"):
        mine, theirs = pl.pallas_call(
            sum_kernel,
            grid_spec=pltpu.PrefetchScalarGridSpec(
                num_scalar_prefetch=2,
                grid=(boards,),
                in_specs=[per_turn((HP, C))],
                out_specs=[whole((4, owners * owned, C))] * 2,
                scratch_shapes=[pltpu.VMEM((buckets, C), F32)] * TABLES,
            ),
            out_shape=[jax.ShapeDtypeStruct((4, owners * owned, C), F32)] * 2,
            compiler_params=params,
            cost_estimate=pl.CostEstimate(
                flops=22 * 10**9, bytes_accessed=10**6, transcendentals=0
            ),
            name="sums",
        )(index, place, delta)
        near = [lax.ppermute(piece, "core", [(0, 1), (1, 0)]) for piece in (plane, up, down)]
        far, theirs, *near = lax.optimization_barrier((far, theirs, *near))
        pieces = [plane, up, far, down, near[0], near[1]]
        pieces += [lax.ppermute(far, "core", [(0, 1), (1, 0)]), near[2]]
        got = lax.ppermute(theirs, "core", [(0, 1), (1, 0)])

    with jax.named_scope("river_sums"):
        chip = mine + got
        columns = lax.all_to_all(chip, "x", 0, 0)
        chip, delta = lax.optimization_barrier((chip, delta))

    with jax.named_scope("replies"):
        replies, gains = pl.pallas_call(
            functools.partial(reply_kernel, turns, rivers, river_total, len(pieces)),
            grid_spec=pltpu.PrefetchScalarGridSpec(
                num_scalar_prefetch=4,
                grid=(turns,),
                in_specs=[
                    per_turn((rivers, H)),
                    whole((turns, H)),
                    per_board((HP, C)),
                    per_turn((HP, C)),
                    whole((G, H)),
                    whole((1, G)),
                    whole((HP, HP)),
                    whole((64, HP)),
                    whole((HP, 256)),
                    whole((8, HP)),
                ]
                + [pl.BlockSpec(memory_space=pl.ANY)] * len(pieces),
                out_specs=[
                    whole((owners, sent_rows, 128)),
                    whole((tbuckets // 2, C)),
                ],
                scratch_shapes=[
                    pltpu.VMEM((rest * devices, C), F32),
                    pltpu.VMEM((2, rivers + 1, HP, C), F32),
                    pltpu.VMEM((HP, C), F32),
                    pltpu.VMEM((C, HP), F32),
                    pltpu.VMEM((8, HP), jnp.int32),
                    pltpu.VMEM((8, HP), jnp.int32),
                    pltpu.VMEM((rivers, HP, C), F32),
                    pltpu.VMEM((rivers, HP, 2 * C), BF),
                    pltpu.VMEM((rivers, 256, C), BF),
                    pltpu.VMEM((HP, C), F32),
                    pltpu.SemaphoreType.DMA((len(pieces),)),
                ],
            ),
            out_shape=[
                jax.ShapeDtypeStruct((owners, sent_rows, 128), F32),
                jax.ShapeDtypeStruct((tbuckets // 2, C), F32),
            ],
            compiler_params=params,
            cost_estimate=pl.CostEstimate(
                flops=30 * 10**9, bytes_accessed=10**6, transcendentals=0
            ),
            name="replies",
        )(
            river_at,
            turn_at,
            turn_card,
            river_at_turn,
            ranks,
            turn_bucket,
            delta,
            bet,
            player_range,
            pot,
            disjoint,
            holds,
            out_of,
            cards,
            *pieces,
        )
    with jax.named_scope("turn_sums"):
        x, core = place[0], place[1]
        pairs = gains.reshape(4, 2, -1, C)
        held = lax.dynamic_index_in_dim(pairs, core, 1, keepdims=False)
        lent = lax.dynamic_index_in_dim(pairs, 1 - core, 1, keepdims=False)
        held = held + lax.ppermute(lent, "core", [(0, 1), (1, 0)])
        turn_parts = [block(held, x)]
        turn_parts += [shifted(block(held, (x + s) % 4), "x", s) for s in (2, 1, 3)]

    with jax.named_scope("exchange"):
        replies, columns, turn_parts = lax.optimization_barrier((replies, columns, turn_parts))
        turn_sums, column = sum(turn_parts[1:], turn_parts[0]), columns.sum(0)
        sent = replies.at[:, turn_row:river_row].set(turn_sums.reshape(owners, -1, 128))
        sent = sent.at[:, river_row:].set(column.reshape(owners, -1, 128))
        came = lax.all_to_all(sent, ("z", "y"), 0, 0)

    with jax.named_scope("update"):
        new_river, new_turn, br_value = pl.pallas_call(
            functools.partial(update_kernel, 1.0 / river_total, each),
            out_shape=[
                jax.ShapeDtypeStruct(river_regret.shape, F32),
                jax.ShapeDtypeStruct(turn_regret.shape, F32),
                jax.ShapeDtypeStruct((turns, each, H), F32),
            ],
            compiler_params=params,
            name="update",
        )(came, river_regret, turn_regret, rperm, tperm)
    return new_river, new_turn, br_value


def solution(mesh):
    mesh = Mesh(mesh.devices.reshape(4, 2, 4, 4), AXES)
    turn, river = AXES[:2], AXES[2:]
    placed = (
        P(AXES, None),
        P(AXES, None),
        P(turn, river, None),
        P(turn, None),
        P(turn, river, None),
        P(turn),
        P(turn, river),
        P(),
        P(),
        P(turn, river, None, None),
        P(),
    )
    return jax.shard_map(
        per_device,
        mesh=mesh,
        in_specs=placed,
        out_specs=(P(AXES, None), P(AXES, None), P(turn, river, None)),
        check_vma=False,
    )
```

```python
import functools

import jax
import jax.numpy as jnp
import ml_dtypes
import numpy as np
from jax import lax
from jax.experimental import pallas as pl
from jax.experimental.pallas import tpu as pltpu
from jax.sharding import Mesh
from jax.sharding import PartitionSpec as P

CARDS = 47
H = CARDS * (CARDS - 1) // 2
HP = 1152
G = 64
C = 2 * G
BF = jnp.bfloat16
F32 = jnp.float32
NT = (((1,), (1,)), ((), ()))
NN = (((1,), (0,)), ((), ()))
TABLES = 6
UNROLL = 47
CHUNKS = 3
INDEX_ROW = 2048
RANKS = 16384.0
AXES = ("x", "core", "z", "y")
VMEM_LIMIT = 60 * 1024 * 1024


def constants():
    first, second = np.triu_indices(CARDS, 1)
    share = (
        (first[:, None] == first[None, :])
        | (first[:, None] == second[None, :])
        | (second[:, None] == first[None, :])
        | (second[:, None] == second[None, :])
    )
    disjoint = np.zeros((HP, HP), np.float32)
    disjoint[:H, :H] = ~share
    cards = np.full((8, HP), -1, np.int32)
    cards[0, :H] = first
    cards[1, :H] = second
    holds = np.zeros((64, HP), np.float32)
    holds[first, np.arange(H)] = 1
    holds[second, np.arange(H)] = 1
    holds[CARDS, :H] = 1
    spread_out = np.zeros((HP, 64), np.float32)
    spread_out[:H, :CARDS] = -holds[:CARDS, :H].T
    spread_out[:H, CARDS] = 1
    spread_out = np.concatenate([spread_out] * 3 + [np.zeros_like(spread_out)], axis=1)
    river_perm = np.zeros((4 * G, 4 * G), np.float32)
    turn_perm = np.zeros((2 * G, 2 * G), np.float32)
    for g in range(G):
        for a in range(2):
            turn_perm[g * 2 + a, a * G + g] = 1
            for b in range(2):
                river_perm[g * 4 + a * 2 + b, b * C + a * G + g] = 1
    halves = [m.astype(ml_dtypes.bfloat16) for m in (disjoint, holds, spread_out, river_perm, turn_perm)]
    return halves + [cards]


def others(x, holds_ref, out_of_ref):
    sums = lax.dot_general(holds_ref[...], x, NN, preferred_element_type=F32)
    pieces = parts(sums, 3)
    pieces = jnp.concatenate(pieces + [jnp.zeros_like(pieces[0])], axis=0)
    return x.astype(F32) + lax.dot_general(
        out_of_ref[...], pieces, NN, preferred_element_type=F32
    )


def parts(x, count):
    out = []
    for _ in range(count):
        piece = x.astype(BF)
        out.append(piece)
        x = x - piece.astype(F32)
    return out


def permuted(x, perm, dims):
    hi, mid, lo = [
        lax.dot_general(piece, perm, dims, preferred_element_type=F32) for piece in parts(x, 3)
    ]
    return (hi + mid) + lo


def first_share(pos0, pos1):
    total = pos0 + pos1
    some = total > 0.0
    safe = jnp.where(some, total, 1.0)
    return jnp.where(some, pos0 / safe, 0.5), jnp.where(some, pos1 / safe, 0.5)


def river_shares(permuted_regret):
    pos = jnp.maximum(permuted_regret, 0.0)
    return first_share(pos[:, :C], pos[:, C:])


def turn_shares(permuted_regret):
    pos = jnp.maximum(permuted_regret, 0.0)
    return first_share(pos, pltpu.roll(pos, G, 1))


def strategy_kernel(
    river_ref,
    turn_ref,
    rperm_ref,
    tperm_ref,
    bucket_ref,
    tbucket_ref,
    out_ref,
    index_ref,
    at_ref,
    tat_ref,
):
    owned, towned = river_ref.shape[0], turn_ref.shape[0]
    rest = owned + towned
    share, _ = river_shares(permuted(river_ref[...], rperm_ref[...], NN))
    tshare, _ = turn_shares(permuted(turn_ref[...], tperm_ref[...], NN))
    for i in range(out_ref.shape[0]):
        out_ref[i, :owned, :] = share
        out_ref[i, owned:, :] = tshare

    turns, rivers, _ = bucket_ref.shape
    index_ref[...] = jnp.zeros_like(index_ref)
    tat_ref[...] = jnp.zeros_like(tat_ref)
    for j in range(HP // 128):
        width = min(128, H - j * 128)
        lanes = slice(j * 128, j * 128 + width)
        for t in range(turns):
            tat_ref[t, j : j + 1, :width] = tbucket_ref[t : t + 1, lanes]
            for r in range(rivers):
                index_ref[t * rivers + r, j : j + 1, :width] = bucket_ref[t, r : r + 1, lanes]

    x, core = lax.axis_index("x"), lax.axis_index("core")

    def placed(bucket, count, offset):
        owner = ((bucket.astype(F32) + 0.5) * (1.0 / count)).astype(jnp.int32)
        row = bucket - owner * count
        other = (core - (owner >> 4)) & 1
        slot = (other * 4 + ((x - (owner >> 5)) & 3)) * 16 + (owner & 15)
        return slot * rest + offset + row

    at_ref[...] = placed(index_ref[...], owned, 0)
    tat_ref[...] = placed(tat_ref[...], towned, owned)


def update_kernel(
    scale, each, came_ref, river_ref, turn_ref, rperm_ref, tperm_ref, river_out, turn_out, br_out
):
    turns = br_out.shape[0]
    blocks = HP // 128
    came = came_ref[0]
    for source in range(1, came_ref.shape[0]):
        came = came + came_ref[source]
    for t in range(turns):
        for j in range(blocks):
            row = (t * blocks + j) * each
            width = min(128, H - j * 128)
            br_out[t, :, j * 128 : j * 128 + width] = came[row : row + each, :width]
    at = turns * blocks * each
    rsum = came[at + 4 : at + 4 + river_ref.shape[0]]
    tsum = came[at : at + 4]
    rp = permuted(river_ref[...], rperm_ref[...], NN)
    s0, s1 = river_shares(rp)
    gain = rsum * scale
    new = jnp.maximum(rp + jnp.concatenate([s1 * gain, -(s0 * gain)], axis=1), 0.0)
    river_out[...] = permuted(new, rperm_ref[...], NT)
    tp = permuted(turn_ref[...], tperm_ref[...], NN)
    _, other = turn_shares(tp)
    lane = lax.broadcasted_iota(jnp.int32, tsum.shape, 1)
    swapped = pltpu.roll(tsum, G, 1)
    low = jnp.where(lane < G, tsum, -swapped)
    high = jnp.where(lane < G, swapped, -tsum)
    gain = jnp.concatenate([low, high], axis=0) * scale
    turn_out[...] = permuted(jnp.maximum(tp + other * gain, 0.0), tperm_ref[...], NT)


def stake_rows(pot_ref):
    pot = pot_ref[...]
    lane = lax.broadcasted_iota(jnp.int32, (1, C), 1)
    bet = 0.5 * jnp.concatenate([pot, pot], axis=1) + jnp.where(lane >= G, 2.0, 0.0)
    return bet * (1.0 / H), (bet + 2.0) * (1.0 / H)


def playable(first, second, turn_value, river_value):
    return (
        (first != turn_value)
        & (second != turn_value)
        & (first != river_value)
        & (second != river_value)
    )


def for_each_hand(index_ref, board, body):
    base = board * INDEX_ROW

    def some(i, _):
        for j in range(UNROLL):
            h = i * UNROLL + j
            body(h, index_ref[base + h], j)
        return 0

    lax.fori_loop(0, H // UNROLL, some, 0)


def widen(wide_s, narrow_ref, out_s):
    wide_s[...] = jnp.zeros_like(wide_s)
    wide_s[:G, :H] = narrow_ref[...]
    wide_s[G:, :H] = narrow_ref[...]
    out_s[...] = jnp.transpose(wide_s[...])


def sign_matrix(rank_ref, r, turn_value, river_value, cards_ref, disjoint_ref, rank_s, signed_s):
    out = jnp.logical_not(
        playable(cards_ref[0:1, :], cards_ref[1:2, :], turn_value, river_value)
    )
    rank_s[r : r + 1, :H] = rank_ref[0, r : r + 1, :]
    rank_row = rank_s[r : r + 1, :].astype(F32) + jnp.where(out, RANKS, 0.0)
    rank_col = jnp.transpose(jnp.broadcast_to(rank_row, (128, HP)))
    for j in range(HP // 128):
        lanes = slice(j * 128, (j + 1) * 128)
        more = (rank_col - rank_row[:, lanes]).astype(BF)
        bound = disjoint_ref[:, lanes]
        signed_s[r, :, lanes] = jnp.maximum(jnp.minimum(more, bound), -bound)
    return rank_col < RANKS


def payoff_kernel(
    rivers,
    start,
    tcard_ref,
    rcard_ref,
    rank_ref,
    call_ref,
    opp_ref,
    pot_ref,
    disjoint_ref,
    holds_ref,
    out_of_ref,
    tperm_ref,
    cards_ref,
    *refs,
):
    (
        delta_ref,
        bet_ref,
        rank_s,
        call_s,
        wide_s,
        opp_s,
        show_s,
        signed_s,
    ) = refs[-8:]
    t = pl.program_id(0) + start

    @pl.when(t == start)
    def _():
        rank_s[...] = jnp.zeros_like(rank_s)
        call_s[rivers * H :, :] = jnp.zeros((rivers * (HP - H), C), F32)
        widen(wide_s, opp_ref, opp_s)

    call_s[: rivers * H, :] = lax.dot_general(
        call_ref[0].reshape(rivers * H, C), tperm_ref[...], NN, preferred_element_type=F32
    )
    low, high = stake_rows(pot_ref)
    bets = 0.0
    for r in range(rivers):
        col_ok = sign_matrix(
            rank_ref, r, tcard_ref[t], rcard_ref[r, t], cards_ref, disjoint_ref, rank_s, signed_s
        )
        called = call_s[pl.ds(r, HP, stride=rivers), :]
        theirs = jnp.where(col_ok, opp_s[...], 0.0)
        show_s[r, :, :C] = theirs.astype(BF)
        show_s[r, :, C:] = (theirs * called).astype(BF)
        show = lax.dot_general(signed_s[r], show_s[r], NN, preferred_element_type=F32)
        fold = others((theirs * (1.0 - called)).astype(BF), holds_ref, out_of_ref)
        bet = jnp.where(col_ok, high * show[:, C:] + low * fold, 0.0)
        delta_ref[r] = jnp.where(col_ok, low * show[:, :C], 0.0) - bet
        bets = bets + bet
    bet_ref[0] = bets


def sum_kernel(index_ref, delta_ref, mine_ref, theirs_ref, *tables):
    board = pl.program_id(0)

    @pl.when(board == 0)
    def _():
        for table in tables:
            table[...] = jnp.zeros_like(table)

    def add_row(h, k, j):
        table = tables[j % TABLES]
        table[pl.ds(k, 1), :] += delta_ref[0, pl.ds(h, 1), :]

    for_each_hand(index_ref, board, add_row)

    @pl.when(board == pl.num_programs(0) - 1)
    def _():
        core = lax.axis_index("core")
        rows = mine_ref.shape[1]
        for s in range(mine_ref.shape[0]):
            for out_ref, c in ((mine_ref, core), (theirs_ref, 1 - core)):
                at = pl.multiple_of((s * 2 + c) * rows, 8)
                total = tables[0][pl.ds(at, rows), :]
                for table in tables[1:]:
                    total = total + table[pl.ds(at, rows), :]
                out_ref[s] = total


def reply_kernel(
    turns,
    rivers,
    river_total,
    pieces,
    bucket_ref,
    tbucket_ref,
    tcard_ref,
    rcard_ref,
    rank_ref,
    trow_ref,
    delta_ref,
    bet_ref,
    mine_ref,
    pot_ref,
    disjoint_ref,
    holds_ref,
    out_of_ref,
    cards_ref,
    *refs,
):
    piece_refs = refs[:pieces]
    (
        out_ref,
        held_ref,
        lent_ref,
        gain_ref,
        table_s,
        rows_s,
        mine_s,
        wide_s,
        rank_s,
        trow_s,
        col_s,
        reach_s,
        sums_s,
        reply_s,
        sem,
    ) = refs[pieces:]
    t = pl.program_id(0)
    now, later = t % 2, (t + 1) % 2
    kinds = rivers + 1

    def take_rows(first, count, turn, slot):
        for j in range(count):
            h = first + j
            k = tbucket_ref[turn * INDEX_ROW + h]
            rows_s[slot, 0, pl.ds(h, 1), :] = table_s[pl.ds(k, 1), :]
            for r in range(rivers):
                k = bucket_ref[(turn * rivers + r) * INDEX_ROW + h]
                rows_s[slot, r + 1, pl.ds(h, 1), :] = table_s[pl.ds(k, 1), :]

    @pl.when(t == 0)
    def _():
        at, copies = 0, []
        for i, piece in enumerate(piece_refs):
            rows = piece.shape[0]
            copies.append(pltpu.make_async_copy(piece, table_s.at[pl.ds(at, rows)], sem.at[i]))
            copies[-1].start()
            at += rows
        rank_s[...] = jnp.zeros_like(rank_s)
        trow_s[...] = jnp.full_like(trow_s, -1)
        gain_ref[...] = jnp.zeros_like(gain_ref)
        widen(wide_s, mine_ref, mine_s)
        for slot in range(2):
            for kind in range(kinds):
                rows_s[slot, kind, H:, :] = jnp.zeros((HP - H, C), F32)
        for copy in copies:
            copy.wait()

        def some(i, _):
            take_rows(i * UNROLL, UNROLL, 0, 0)
            return 0

        lax.fori_loop(0, H // UNROLL, some, 0)

    low, high = stake_rows(pot_ref)
    reach = mine_s[...] * rows_s[now, 0]
    nodes = bet_ref[0]
    for r in range(rivers):
        first = rows_s[now, r + 1]
        out = jnp.logical_not(
            playable(cards_ref[0:1, :], cards_ref[1:2, :], tcard_ref[t], rcard_ref[r, t])
        )
        rank_s[r : r + 1, :H] = rank_ref[0, r : r + 1, :]
        rank_row = rank_s[r : r + 1, :].astype(F32) + jnp.where(out, RANKS, 0.0)
        col_s[r] = jnp.transpose(jnp.broadcast_to(rank_row, (128, HP)))
        col_ok = col_s[r] < RANKS
        reach_s[r, :, :C] = jnp.where(col_ok, reach * first, 0.0).astype(BF)
        reach_s[r, :, C:] = jnp.where(col_ok, reach * (1.0 - first), 0.0).astype(BF)
        sums = lax.dot_general(
            holds_ref[...], reach_s[r, :, C:], NN, preferred_element_type=F32
        )
        split = parts(sums, 3)
        sums_s[r] = jnp.concatenate(split + [jnp.zeros_like(split[0])], axis=0)
        nodes = nodes + first * delta_ref[r]
    rank_rows = [
        rank_s[r : r + 1, :].astype(F32)
        + jnp.where(
            playable(cards_ref[0:1, :], cards_ref[1:2, :], tcard_ref[t], rcard_ref[r, t]),
            0.0,
            RANKS,
        )
        for r in range(rivers)
    ]

    def some_replies(at, count):
        rows = pl.ds(at, count)
        total = 0.0
        for r in range(rivers):
            col = col_s[r, rows, :]
            signed = []
            for j in range(HP // 128):
                lanes = slice(j * 128, (j + 1) * 128)
                more = (col - rank_rows[r][:, lanes]).astype(BF)
                bound = disjoint_ref[rows, lanes]
                signed.append(jnp.maximum(jnp.minimum(more, bound), -bound))
            against = lax.dot_general(
                jnp.concatenate(signed, axis=1), reach_s[r], NN, preferred_element_type=F32
            )
            against_bet = reach_s[r, rows, C:].astype(F32) + lax.dot_general(
                out_of_ref[rows, :], sums_s[r], NN, preferred_element_type=F32
            )
            reply = low * against[:, :C] + jnp.maximum(
                high * against[:, C:], -(low * against_bet)
            )
            total = total + jnp.where(col < RANKS, reply, 0.0)
        reply_s[rows, :] = total

    chunk = HP // CHUNKS
    taken = -(-H // CHUNKS)

    def with_rows(i, _):
        take_rows(i * taken, taken, t + 1, later)
        some_replies(pl.multiple_of(i * chunk, 128), chunk)
        return 0

    def without_rows(i, _):
        some_replies(pl.multiple_of(i * chunk, 128), chunk)
        return 0

    @pl.when(t < turns - 1)
    def _():
        lax.fori_loop(0, CHUNKS, with_rows, 0)

    @pl.when(t == turns - 1)
    def _():
        lax.fori_loop(0, CHUNKS, without_rows, 0)

    hi, lo = parts(nodes - pltpu.roll(nodes, G, 1), 2)
    both = jnp.concatenate([hi[:, :G], lo[:, :G]], axis=1)
    trow_s[0:1, :H] = trow_ref[pl.ds(t, 1), :]
    trow = trow_s[0:1, :]
    row = lax.broadcasted_iota(jnp.int32, (gain_ref.shape[0], HP), 0)
    bucket = row // 4 * 8 + row % 4

    def sums_of(ids):
        hot = jnp.where(ids == trow, 1.0, 0.0).astype(BF)
        out = lax.dot_general(hot, both, NN, preferred_element_type=F32)
        return out + pltpu.roll(out, G, 1)

    lane = lax.broadcasted_iota(jnp.int32, gain_ref.shape, 1)
    gain_ref[...] += jnp.where(lane < G, sums_of(bucket), sums_of(bucket + 4))

    @pl.when(t == turns - 1)
    def _():
        x, core = lax.axis_index("x"), lax.axis_index("core")
        ring, count, _ = held_ref.shape
        for s in range(ring):
            for part_ref, c in ((held_ref, core), (lent_ref, 1 - core)):
                at = pl.multiple_of((((x + s) & 3) * 2 + c) * count, 8)
                part_ref[s] = gain_ref[pl.ds(at, count), :]

    flat = jnp.transpose(reply_s[...])
    flat = (flat[:G] + flat[G:]) * (1.0 / river_total)
    owners = out_ref.shape[0]
    each = G // owners
    blocks = HP // 128
    for turn in range(turns):

        @pl.when(t == turn)
        def _():
            for j in range(blocks):
                piece = flat[:, j * 128 : (j + 1) * 128].reshape(owners, each, 128)
                row = (turn * blocks + j) * each
                out_ref[:, row : row + each, :] = piece


def shifted(x, axis, shift):
    return lax.ppermute(x, axis, [(i, (i + shift) % 4) for i in range(4)])


def per_device(
    river_regret,
    turn_regret,
    river_bucket,
    turn_bucket,
    ranks,
    turn_card,
    river_card,
    player_range,
    opp_range,
    call_prob,
    base_pot,
):
    turns, rivers, _ = river_bucket.shape
    boards = turns * rivers
    devices = 128
    owners = 16
    each = G // owners
    river_total = rivers * owners
    owned, towned = river_regret.shape[0], turn_regret.shape[0]
    buckets, tbuckets = owned * devices, towned * devices
    disjoint, holds, out_of, rperm, tperm, cards = constants()
    params = pltpu.CompilerParams(vmem_limit_bytes=VMEM_LIMIT)
    pot = base_pot.reshape(1, G)
    calls = jnp.transpose(call_prob, (0, 3, 1, 2))
    river_at_turn = river_card.T
    rest = owned + towned
    swap = [(0, 1), (1, 0)]
    turn_row = turns * (HP // 128) * each
    river_row = turn_row + towned // 2
    sent_rows = river_row + owned

    with jax.named_scope("strategies"):
        strategies, *indices = pl.pallas_call(
            strategy_kernel,
            out_shape=[
                jax.ShapeDtypeStruct((owners, rest, C), F32),
                jax.ShapeDtypeStruct((boards, INDEX_ROW // 128, 128), jnp.int32),
                jax.ShapeDtypeStruct((boards, INDEX_ROW // 128, 128), jnp.int32),
                jax.ShapeDtypeStruct((turns, INDEX_ROW // 128, 128), jnp.int32),
            ],
            compiler_params=params,
            name="strategies",
        )(river_regret, turn_regret, rperm, tperm, river_bucket, turn_bucket)
        index, river_at, turn_at = (a.reshape(-1) for a in indices)
        plane = lax.all_to_all(strategies, ("z", "y"), 0, 0).reshape(-1, C)

    def whole(shape):
        return pl.BlockSpec(shape, lambda i, *_: (0,) * len(shape))

    def per_turn(shape, count=1):
        return pl.BlockSpec((count,) + shape, lambda i, *_: (i,) + (0,) * len(shape))

    def per_board(shape):
        return per_turn(shape, rivers)

    def payoffs(start, count, known=()):
        def of_turn(shape, each_turn=1):
            return pl.BlockSpec(
                (each_turn,) + shape, lambda i, *_: (i + start,) + (0,) * len(shape)
            )

        return pl.pallas_call(
            functools.partial(payoff_kernel, rivers, start),
            grid_spec=pltpu.PrefetchScalarGridSpec(
                num_scalar_prefetch=2,
                grid=(count,),
                in_specs=[
                    of_turn((rivers, H)),
                    of_turn((H, rivers, C)),
                    whole((G, H)),
                    whole((1, G)),
                    whole((HP, HP)),
                    whole((64, HP)),
                    whole((HP, 256)),
                    whole((C, C)),
                    whole((8, HP)),
                ]
                + [pl.BlockSpec(memory_space=pl.ANY)] * len(known),
                out_specs=[of_turn((HP, C), rivers), of_turn((HP, C))],
                scratch_shapes=[
                    pltpu.VMEM((8, HP), jnp.int32),
                    pltpu.VMEM((rivers * HP, C), F32),
                    pltpu.VMEM((C, HP), F32),
                    pltpu.VMEM((HP, C), F32),
                    pltpu.VMEM((rivers, HP, 2 * C), BF),
                    pltpu.VMEM((rivers, HP, HP), BF),
                ],
            ),
            out_shape=[
                jax.ShapeDtypeStruct((boards, HP, C), F32),
                jax.ShapeDtypeStruct((turns, HP, C), F32),
            ],
            input_output_aliases={11 + i: i for i in range(len(known))},
            compiler_params=params,
            cost_estimate=pl.CostEstimate(
                flops=count * 8 * 10**9, bytes_accessed=10**6, transcendentals=0
            ),
            name="payoffs",
        )(
            turn_card,
            river_at_turn,
            ranks,
            calls,
            opp_range,
            pot,
            disjoint,
            holds,
            out_of,
            tperm,
            cards,
            *known,
        )

    with jax.named_scope("payoffs"):
        delta, bet = payoffs(0, turns)
    with jax.named_scope("strategies"):
        plane, delta = lax.optimization_barrier((plane, delta))
        up, down = shifted(plane, "x", 1), shifted(plane, "x", 3)

    with jax.named_scope("river_sums"):
        mine, theirs = pl.pallas_call(
            sum_kernel,
            grid_spec=pltpu.PrefetchScalarGridSpec(
                num_scalar_prefetch=1,
                grid=(boards,),
                in_specs=[per_turn((HP, C))],
                out_specs=[whole((4, owners * owned, C))] * 2,
                scratch_shapes=[pltpu.VMEM((buckets, C), F32)] * TABLES,
            ),
            out_shape=[jax.ShapeDtypeStruct((4, owners * owned, C), F32)] * 2,
            compiler_params=params,
            cost_estimate=pl.CostEstimate(
                flops=22 * 10**9, bytes_accessed=10**6, transcendentals=0
            ),
            name="sums",
        )(index, delta)
        up, down, theirs = lax.optimization_barrier((up, down, theirs))
        got = lax.ppermute(theirs, "core", swap)
        half = up.shape[0] // 2
        far = [shifted(up[:half], "x", 1), shifted(down[half:], "x", 3)]
        chip = mine + got
        chip, *far = lax.optimization_barrier((chip, *far))
        columns = lax.all_to_all(chip, "x", 0, 0)
        own = [plane, up, *far, down]
        pieces = own + [lax.ppermute(piece, "core", swap) for piece in own]
        delta, chip, *pieces = lax.optimization_barrier((delta, chip, *pieces))

    with jax.named_scope("replies"):
        replies, held, lent = pl.pallas_call(
            functools.partial(reply_kernel, turns, rivers, river_total, len(pieces)),
            grid_spec=pltpu.PrefetchScalarGridSpec(
                num_scalar_prefetch=4,
                grid=(turns,),
                in_specs=[
                    per_turn((rivers, H)),
                    whole((turns, H)),
                    per_board((HP, C)),
                    per_turn((HP, C)),
                    whole((G, H)),
                    whole((1, G)),
                    whole((HP, HP)),
                    whole((64, HP)),
                    whole((HP, 256)),
                    whole((8, HP)),
                ]
                + [pl.BlockSpec(memory_space=pl.ANY)] * len(pieces),
                out_specs=[
                    whole((owners, sent_rows, 128)),
                    whole((4, owners * towned // 2, C)),
                    whole((4, owners * towned // 2, C)),
                ],
                scratch_shapes=[
                    pltpu.VMEM((tbuckets // 2, C), F32),
                    pltpu.VMEM((rest * devices, C), F32),
                    pltpu.VMEM((2, rivers + 1, HP, C), F32),
                    pltpu.VMEM((HP, C), F32),
                    pltpu.VMEM((C, HP), F32),
                    pltpu.VMEM((8, HP), jnp.int32),
                    pltpu.VMEM((8, HP), jnp.int32),
                    pltpu.VMEM((rivers, HP, C), F32),
                    pltpu.VMEM((rivers, HP, 2 * C), BF),
                    pltpu.VMEM((rivers, 256, C), BF),
                    pltpu.VMEM((HP, C), F32),
                    pltpu.SemaphoreType.DMA((len(pieces),)),
                ],
            ),
            out_shape=[
                jax.ShapeDtypeStruct((owners, sent_rows, 128), F32),
                jax.ShapeDtypeStruct((4, owners * towned // 2, C), F32),
                jax.ShapeDtypeStruct((4, owners * towned // 2, C), F32),
            ],
            compiler_params=params,
            cost_estimate=pl.CostEstimate(
                flops=30 * 10**9, bytes_accessed=10**6, transcendentals=0
            ),
            name="replies",
        )(
            river_at,
            turn_at,
            turn_card,
            river_at_turn,
            ranks,
            turn_bucket,
            delta,
            bet,
            player_range,
            pot,
            disjoint,
            holds,
            out_of,
            cards,
            *pieces,
        )
    with jax.named_scope("turn_sums"):
        held = held + lax.ppermute(lent, "core", swap)
        turn_parts = [held[0]] + [shifted(held[s], "x", s) for s in (2, 1, 3)]

    with jax.named_scope("exchange"):
        replies, columns, turn_parts = lax.optimization_barrier((replies, columns, turn_parts))
        turn_sums, column = sum(turn_parts[1:], turn_parts[0]), columns.sum(0)
        sent = replies.at[:, turn_row:river_row].set(turn_sums.reshape(owners, -1, 128))
        sent = sent.at[:, river_row:].set(column.reshape(owners, -1, 128))
        came = lax.all_to_all(sent, ("z", "y"), 0, 0)

    with jax.named_scope("update"):
        new_river, new_turn, br_value = pl.pallas_call(
            functools.partial(update_kernel, 1.0 / river_total, each),
            out_shape=[
                jax.ShapeDtypeStruct(river_regret.shape, F32),
                jax.ShapeDtypeStruct(turn_regret.shape, F32),
                jax.ShapeDtypeStruct((turns, each, H), F32),
            ],
            compiler_params=params,
            name="update",
        )(came, river_regret, turn_regret, rperm, tperm)
    return new_river, new_turn, br_value


def solution(mesh):
    mesh = Mesh(mesh.devices.reshape(4, 2, 4, 4), AXES)
    turn, river = AXES[:2], AXES[2:]
    placed = (
        P(AXES, None),
        P(AXES, None),
        P(turn, river, None),
        P(turn, None),
        P(turn, river, None),
        P(turn),
        P(turn, river),
        P(),
        P(),
        P(turn, river, None, None),
        P(),
    )
    return jax.shard_map(
        per_device,
        mesh=mesh,
        in_specs=placed,
        out_specs=(P(AXES, None), P(AXES, None), P(turn, river, None)),
        check_vma=False,
    )
```

```python
import functools

import jax
import jax.numpy as jnp
import ml_dtypes
import numpy as np
from jax import lax
from jax.experimental import pallas as pl
from jax.experimental.pallas import tpu as pltpu
from jax.sharding import Mesh
from jax.sharding import PartitionSpec as P

CARDS = 47
H = CARDS * (CARDS - 1) // 2
HP = 1152
G = 64
C = 2 * G
BF = jnp.bfloat16
F32 = jnp.float32
NT = (((1,), (1,)), ((), ()))
NN = (((1,), (0,)), ((), ()))
TABLES = 6
UNROLL = 47
INDEX_ROW = 2048
RANKS = 16384.0
AXES = ("x", "core", "z", "y")
VMEM_LIMIT = 60 * 1024 * 1024


def constants():
    first, second = np.triu_indices(CARDS, 1)
    share = (
        (first[:, None] == first[None, :])
        | (first[:, None] == second[None, :])
        | (second[:, None] == first[None, :])
        | (second[:, None] == second[None, :])
    )
    disjoint = np.zeros((HP, HP), np.float32)
    disjoint[:H, :H] = ~share
    cards = np.full((8, HP), -1, np.int32)
    cards[0, :H] = first
    cards[1, :H] = second
    holds = np.zeros((64, HP), np.float32)
    holds[first, np.arange(H)] = 1
    holds[second, np.arange(H)] = 1
    holds[CARDS, :H] = 1
    spread_out = np.zeros((HP, 64), np.float32)
    spread_out[:H, :CARDS] = -holds[:CARDS, :H].T
    spread_out[:H, CARDS] = 1
    spread_out = np.concatenate([spread_out] * 3 + [np.zeros_like(spread_out)], axis=1)
    river_perm = np.zeros((4 * G, 4 * G), np.float32)
    turn_perm = np.zeros((2 * G, 2 * G), np.float32)
    for g in range(G):
        for a in range(2):
            turn_perm[g * 2 + a, a * G + g] = 1
            for b in range(2):
                river_perm[g * 4 + a * 2 + b, b * C + a * G + g] = 1
    halves = [m.astype(ml_dtypes.bfloat16) for m in (disjoint, holds, spread_out, river_perm, turn_perm)]
    return halves + [cards]


def others(x, holds_ref, out_of_ref):
    sums = lax.dot_general(holds_ref[...], x, NN, preferred_element_type=F32)
    pieces = parts(sums, 3)
    pieces = jnp.concatenate(pieces + [jnp.zeros_like(pieces[0])], axis=0)
    return x.astype(F32) + lax.dot_general(
        out_of_ref[...], pieces, NN, preferred_element_type=F32
    )


def parts(x, count):
    out = []
    for _ in range(count):
        piece = x.astype(BF)
        out.append(piece)
        x = x - piece.astype(F32)
    return out


def permuted(x, perm, dims):
    hi, mid, lo = [
        lax.dot_general(piece, perm, dims, preferred_element_type=F32) for piece in parts(x, 3)
    ]
    return (hi + mid) + lo


def first_share(pos0, pos1):
    total = pos0 + pos1
    some = total > 0.0
    safe = jnp.where(some, total, 1.0)
    return jnp.where(some, pos0 / safe, 0.5), jnp.where(some, pos1 / safe, 0.5)


def river_shares(permuted_regret):
    pos = jnp.maximum(permuted_regret, 0.0)
    return first_share(pos[:, :C], pos[:, C:])


def turn_shares(permuted_regret):
    pos = jnp.maximum(permuted_regret, 0.0)
    return first_share(pos, pltpu.roll(pos, G, 1))


def strategy_kernel(
    river_ref,
    turn_ref,
    rperm_ref,
    tperm_ref,
    bucket_ref,
    tbucket_ref,
    out_ref,
    index_ref,
    at_ref,
    tat_ref,
):
    owned, towned = river_ref.shape[0], turn_ref.shape[0]
    rest = owned + towned
    share, _ = river_shares(permuted(river_ref[...], rperm_ref[...], NN))
    tshare, _ = turn_shares(permuted(turn_ref[...], tperm_ref[...], NN))
    for i in range(out_ref.shape[0]):
        out_ref[i, :owned, :] = share
        out_ref[i, owned:, :] = tshare

    turns, rivers, _ = bucket_ref.shape
    index_ref[...] = jnp.zeros_like(index_ref)
    tat_ref[...] = jnp.zeros_like(tat_ref)
    for j in range(HP // 128):
        width = min(128, H - j * 128)
        lanes = slice(j * 128, j * 128 + width)
        for t in range(turns):
            tat_ref[t, j : j + 1, :width] = tbucket_ref[t : t + 1, lanes]
            for r in range(rivers):
                index_ref[t * rivers + r, j : j + 1, :width] = bucket_ref[t, r : r + 1, lanes]

    x, core = lax.axis_index("x"), lax.axis_index("core")

    def placed(bucket, count, offset):
        owner = ((bucket.astype(F32) + 0.5) * (1.0 / count)).astype(jnp.int32)
        row = bucket - owner * count
        other = (core - (owner >> 4)) & 1
        slot = (other * 4 + ((x - (owner >> 5)) & 3)) * 16 + (owner & 15)
        return slot * rest + offset + row

    at_ref[...] = placed(index_ref[...], owned, 0)
    tat_ref[...] = placed(tat_ref[...], towned, owned)


def update_kernel(
    scale, each, came_ref, river_ref, turn_ref, rperm_ref, tperm_ref, river_out, turn_out, br_out
):
    turns = br_out.shape[0]
    blocks = HP // 128
    came = came_ref[0]
    for source in range(1, came_ref.shape[0]):
        came = came + came_ref[source]
    for t in range(turns):
        for j in range(blocks):
            row = (t * blocks + j) * each
            width = min(128, H - j * 128)
            br_out[t, :, j * 128 : j * 128 + width] = came[row : row + each, :width]
    at = turns * blocks * each
    rsum = came[at + 4 : at + 4 + river_ref.shape[0]]
    tsum = came[at : at + 4]
    rp = permuted(river_ref[...], rperm_ref[...], NN)
    s0, s1 = river_shares(rp)
    gain = rsum * scale
    new = jnp.maximum(rp + jnp.concatenate([s1 * gain, -(s0 * gain)], axis=1), 0.0)
    river_out[...] = permuted(new, rperm_ref[...], NT)
    tp = permuted(turn_ref[...], tperm_ref[...], NN)
    _, other = turn_shares(tp)
    lane = lax.broadcasted_iota(jnp.int32, tsum.shape, 1)
    swapped = pltpu.roll(tsum, G, 1)
    low = jnp.where(lane < G, tsum, -swapped)
    high = jnp.where(lane < G, swapped, -tsum)
    gain = jnp.concatenate([low, high], axis=0) * scale
    turn_out[...] = permuted(jnp.maximum(tp + other * gain, 0.0), tperm_ref[...], NT)


def stake_rows(pot_ref):
    pot = pot_ref[...]
    lane = lax.broadcasted_iota(jnp.int32, (1, C), 1)
    bet = 0.5 * jnp.concatenate([pot, pot], axis=1) + jnp.where(lane >= G, 2.0, 0.0)
    return bet * (1.0 / H), (bet + 2.0) * (1.0 / H)


def playable(first, second, turn_value, river_value):
    return (
        (first != turn_value)
        & (second != turn_value)
        & (first != river_value)
        & (second != river_value)
    )


def for_each_hand(index_ref, board, body):
    base = board * INDEX_ROW

    def some(i, _):
        for j in range(UNROLL):
            h = i * UNROLL + j
            body(h, index_ref[base + h], j)
        return 0

    lax.fori_loop(0, H // UNROLL, some, 0)


def widen(wide_s, narrow_ref, out_s):
    wide_s[...] = jnp.zeros_like(wide_s)
    wide_s[:G, :H] = narrow_ref[...]
    wide_s[G:, :H] = narrow_ref[...]
    out_s[...] = jnp.transpose(wide_s[...])


def sign_matrix(rank_ref, r, turn_value, river_value, cards_ref, disjoint_ref, rank_s):
    out = jnp.logical_not(
        playable(cards_ref[0:1, :], cards_ref[1:2, :], turn_value, river_value)
    )
    rank_s[r : r + 1, :H] = rank_ref[0, r : r + 1, :]
    rank_row = rank_s[r : r + 1, :].astype(F32) + jnp.where(out, RANKS, 0.0)
    rank_col = jnp.transpose(jnp.broadcast_to(rank_row, (128, HP)))
    signed = []
    for j in range(HP // 128):
        lanes = slice(j * 128, (j + 1) * 128)
        more = (rank_col - rank_row[:, lanes]).astype(BF)
        bound = disjoint_ref[:, lanes]
        signed.append(jnp.maximum(jnp.minimum(more, bound), -bound))
    return rank_col < RANKS, jnp.concatenate(signed, axis=1)


def payoff_kernel(
    rivers,
    start,
    tcard_ref,
    rcard_ref,
    rank_ref,
    call_ref,
    opp_ref,
    pot_ref,
    disjoint_ref,
    holds_ref,
    out_of_ref,
    tperm_ref,
    cards_ref,
    *refs,
):
    (
        delta_ref,
        bet_ref,
        rank_s,
        call_s,
        wide_s,
        opp_s,
        show_s,
    ) = refs[-7:]
    t = pl.program_id(0) + start

    @pl.when(t == start)
    def _():
        rank_s[...] = jnp.zeros_like(rank_s)
        call_s[rivers * H :, :] = jnp.zeros((rivers * (HP - H), C), F32)
        widen(wide_s, opp_ref, opp_s)

    call_s[: rivers * H, :] = lax.dot_general(
        call_ref[0].reshape(rivers * H, C), tperm_ref[...], NN, preferred_element_type=F32
    )
    low, high = stake_rows(pot_ref)
    bets = 0.0
    for r in range(rivers):
        col_ok, signed = sign_matrix(
            rank_ref, r, tcard_ref[t], rcard_ref[r, t], cards_ref, disjoint_ref, rank_s
        )
        called = call_s[pl.ds(r, HP, stride=rivers), :]
        theirs = jnp.where(col_ok, opp_s[...], 0.0)
        show_s[r, :, :C] = theirs.astype(BF)
        show_s[r, :, C:] = (theirs * called).astype(BF)
        show = lax.dot_general(signed, show_s[r], NN, preferred_element_type=F32)
        fold = others((theirs * (1.0 - called)).astype(BF), holds_ref, out_of_ref)
        bet = jnp.where(col_ok, high * show[:, C:] + low * fold, 0.0)
        delta_ref[r] = jnp.where(col_ok, low * show[:, :C], 0.0) - bet
        bets = bets + bet
    bet_ref[0] = bets


def sum_kernel(index_ref, delta_ref, mine_ref, theirs_ref, *tables):
    board = pl.program_id(0)

    @pl.when(board == 0)
    def _():
        for table in tables:
            table[...] = jnp.zeros_like(table)

    def add_row(h, k, j):
        table = tables[j % TABLES]
        table[pl.ds(k, 1), :] += delta_ref[0, pl.ds(h, 1), :]

    for_each_hand(index_ref, board, add_row)

    @pl.when(board == pl.num_programs(0) - 1)
    def _():
        core = lax.axis_index("core")
        rows = mine_ref.shape[1]
        for s in range(mine_ref.shape[0]):
            for out_ref, c in ((mine_ref, core), (theirs_ref, 1 - core)):
                at = pl.multiple_of((s * 2 + c) * rows, 8)
                total = tables[0][pl.ds(at, rows), :]
                for table in tables[1:]:
                    total = total + table[pl.ds(at, rows), :]
                out_ref[s] = total


def reply_kernel(
    turns,
    rivers,
    river_total,
    pieces,
    bucket_ref,
    tbucket_ref,
    tcard_ref,
    rcard_ref,
    rank_ref,
    trow_ref,
    delta_ref,
    bet_ref,
    mine_ref,
    pot_ref,
    disjoint_ref,
    holds_ref,
    out_of_ref,
    cards_ref,
    *refs,
):
    piece_refs = refs[:pieces]
    (
        out_ref,
        held_ref,
        lent_ref,
        gain_ref,
        table_s,
        rows_s,
        mine_s,
        wide_s,
        rank_s,
        trow_s,
        col_s,
        reach_s,
        sums_s,
        reply_s,
        sem,
    ) = refs[pieces:]
    t = pl.program_id(0)
    now, later = t % 2, (t + 1) % 2
    kinds = rivers + 1

    def take_rows(first, count, turn, slot):
        for j in range(count):
            h = first + j
            k = tbucket_ref[turn * INDEX_ROW + h]
            rows_s[slot, 0, pl.ds(h, 1), :] = table_s[pl.ds(k, 1), :]
            for r in range(rivers):
                k = bucket_ref[(turn * rivers + r) * INDEX_ROW + h]
                rows_s[slot, r + 1, pl.ds(h, 1), :] = table_s[pl.ds(k, 1), :]

    @pl.when(t == 0)
    def _():
        at, copies = 0, []
        for i, piece in enumerate(piece_refs):
            rows = piece.shape[0]
            copies.append(pltpu.make_async_copy(piece, table_s.at[pl.ds(at, rows)], sem.at[i]))
            copies[-1].start()
            at += rows
        rank_s[...] = jnp.zeros_like(rank_s)
        trow_s[...] = jnp.full_like(trow_s, -1)
        gain_ref[...] = jnp.zeros_like(gain_ref)
        widen(wide_s, mine_ref, mine_s)
        for slot in range(2):
            for kind in range(kinds):
                rows_s[slot, kind, H:, :] = jnp.zeros((HP - H, C), F32)
        for copy in copies:
            copy.wait()

        def some(i, _):
            take_rows(i * UNROLL, UNROLL, 0, 0)
            return 0

        lax.fori_loop(0, H // UNROLL, some, 0)

    low, high = stake_rows(pot_ref)
    reach = mine_s[...] * rows_s[now, 0]
    nodes = bet_ref[0]
    for r in range(rivers):
        first = rows_s[now, r + 1]
        out = jnp.logical_not(
            playable(cards_ref[0:1, :], cards_ref[1:2, :], tcard_ref[t], rcard_ref[r, t])
        )
        rank_s[r : r + 1, :H] = rank_ref[0, r : r + 1, :]
        rank_row = rank_s[r : r + 1, :].astype(F32) + jnp.where(out, RANKS, 0.0)
        col_s[r] = jnp.transpose(jnp.broadcast_to(rank_row, (128, HP)))
        col_ok = col_s[r] < RANKS
        reach_s[r, :, :C] = jnp.where(col_ok, reach * first, 0.0).astype(BF)
        reach_s[r, :, C:] = jnp.where(col_ok, reach * (1.0 - first), 0.0).astype(BF)
        sums = lax.dot_general(
            holds_ref[...], reach_s[r, :, C:], NN, preferred_element_type=F32
        )
        split = parts(sums, 3)
        sums_s[r] = jnp.concatenate(split + [jnp.zeros_like(split[0])], axis=0)
        nodes = nodes + first * delta_ref[r]
    rank_rows = [
        rank_s[r : r + 1, :].astype(F32)
        + jnp.where(
            playable(cards_ref[0:1, :], cards_ref[1:2, :], tcard_ref[t], rcard_ref[r, t]),
            0.0,
            RANKS,
        )
        for r in range(rivers)
    ]

    def some_replies(at, count):
        rows = pl.ds(at, count)
        total = 0.0
        for r in range(rivers):
            col = col_s[r, rows, :]
            signed = []
            for j in range(HP // 128):
                lanes = slice(j * 128, (j + 1) * 128)
                more = (col - rank_rows[r][:, lanes]).astype(BF)
                bound = disjoint_ref[rows, lanes]
                signed.append(jnp.maximum(jnp.minimum(more, bound), -bound))
            against = lax.dot_general(
                jnp.concatenate(signed, axis=1), reach_s[r], NN, preferred_element_type=F32
            )
            against_bet = reach_s[r, rows, C:].astype(F32) + lax.dot_general(
                out_of_ref[rows, :], sums_s[r], NN, preferred_element_type=F32
            )
            reply = low * against[:, :C] + jnp.maximum(
                high * against[:, C:], -(low * against_bet)
            )
            total = total + jnp.where(col < RANKS, reply, 0.0)
        reply_s[rows, :] = total


    some_replies(0, HP)

    hi, lo = parts(nodes - pltpu.roll(nodes, G, 1), 2)
    both = jnp.concatenate([hi[:, :G], lo[:, :G]], axis=1)
    trow_s[0:1, :H] = trow_ref[pl.ds(t, 1), :]
    trow = trow_s[0:1, :]
    row = lax.broadcasted_iota(jnp.int32, (gain_ref.shape[0], HP), 0)
    bucket = row // 4 * 8 + row % 4

    def sums_of(ids):
        hot = jnp.where(ids == trow, 1.0, 0.0).astype(BF)
        out = lax.dot_general(hot, both, NN, preferred_element_type=F32)
        return out + pltpu.roll(out, G, 1)

    lane = lax.broadcasted_iota(jnp.int32, gain_ref.shape, 1)
    gain_ref[...] += jnp.where(lane < G, sums_of(bucket), sums_of(bucket + 4))

    @pl.when(t == turns - 1)
    def _():
        x, core = lax.axis_index("x"), lax.axis_index("core")
        ring, count, _ = held_ref.shape
        for s in range(ring):
            for part_ref, c in ((held_ref, core), (lent_ref, 1 - core)):
                at = pl.multiple_of((((x + s) & 3) * 2 + c) * count, 8)
                part_ref[s] = gain_ref[pl.ds(at, count), :]

    @pl.when(t < turns - 1)
    def _():
        def some(i, _):
            take_rows(i * UNROLL, UNROLL, t + 1, later)
            return 0

        lax.fori_loop(0, H // UNROLL, some, 0)

    flat = jnp.transpose(reply_s[...])
    flat = (flat[:G] + flat[G:]) * (1.0 / river_total)
    owners = out_ref.shape[0]
    each = G // owners
    blocks = HP // 128
    for turn in range(turns):

        @pl.when(t == turn)
        def _():
            for j in range(blocks):
                piece = flat[:, j * 128 : (j + 1) * 128].reshape(owners, each, 128)
                row = (turn * blocks + j) * each
                out_ref[:, row : row + each, :] = piece


def shifted(x, axis, shift):
    return lax.ppermute(x, axis, [(i, (i + shift) % 4) for i in range(4)])


def per_device(
    river_regret,
    turn_regret,
    river_bucket,
    turn_bucket,
    ranks,
    turn_card,
    river_card,
    player_range,
    opp_range,
    call_prob,
    base_pot,
):
    turns, rivers, _ = river_bucket.shape
    boards = turns * rivers
    devices = 128
    owners = 16
    each = G // owners
    river_total = rivers * owners
    owned, towned = river_regret.shape[0], turn_regret.shape[0]
    buckets, tbuckets = owned * devices, towned * devices
    disjoint, holds, out_of, rperm, tperm, cards = constants()
    params = pltpu.CompilerParams(vmem_limit_bytes=VMEM_LIMIT)
    pot = base_pot.reshape(1, G)
    calls = jnp.transpose(call_prob, (0, 3, 1, 2))
    river_at_turn = river_card.T
    rest = owned + towned
    swap = [(0, 1), (1, 0)]
    turn_row = turns * (HP // 128) * each
    river_row = turn_row + towned // 2
    sent_rows = river_row + owned

    with jax.named_scope("strategies"):
        strategies, *indices = pl.pallas_call(
            strategy_kernel,
            out_shape=[
                jax.ShapeDtypeStruct((owners, rest, C), F32),
                jax.ShapeDtypeStruct((boards, INDEX_ROW // 128, 128), jnp.int32),
                jax.ShapeDtypeStruct((boards, INDEX_ROW // 128, 128), jnp.int32),
                jax.ShapeDtypeStruct((turns, INDEX_ROW // 128, 128), jnp.int32),
            ],
            compiler_params=params,
            name="strategies",
        )(river_regret, turn_regret, rperm, tperm, river_bucket, turn_bucket)
        index, river_at, turn_at = (a.reshape(-1) for a in indices)
        plane = lax.all_to_all(strategies, ("z", "y"), 0, 0).reshape(-1, C)

    def whole(shape):
        return pl.BlockSpec(shape, lambda i, *_: (0,) * len(shape))

    def per_turn(shape, count=1):
        return pl.BlockSpec((count,) + shape, lambda i, *_: (i,) + (0,) * len(shape))

    def per_board(shape):
        return per_turn(shape, rivers)

    def payoffs(start, count, known=()):
        def of_turn(shape, each_turn=1):
            return pl.BlockSpec(
                (each_turn,) + shape, lambda i, *_: (i + start,) + (0,) * len(shape)
            )

        return pl.pallas_call(
            functools.partial(payoff_kernel, rivers, start),
            grid_spec=pltpu.PrefetchScalarGridSpec(
                num_scalar_prefetch=2,
                grid=(count,),
                in_specs=[
                    of_turn((rivers, H)),
                    of_turn((H, rivers, C)),
                    whole((G, H)),
                    whole((1, G)),
                    whole((HP, HP)),
                    whole((64, HP)),
                    whole((HP, 256)),
                    whole((C, C)),
                    whole((8, HP)),
                ]
                + [pl.BlockSpec(memory_space=pl.ANY)] * len(known),
                out_specs=[of_turn((HP, C), rivers), of_turn((HP, C))],
                scratch_shapes=[
                    pltpu.VMEM((8, HP), jnp.int32),
                    pltpu.VMEM((rivers * HP, C), F32),
                    pltpu.VMEM((C, HP), F32),
                    pltpu.VMEM((HP, C), F32),
                    pltpu.VMEM((rivers, HP, 2 * C), BF),
                ],
            ),
            out_shape=[
                jax.ShapeDtypeStruct((boards, HP, C), F32),
                jax.ShapeDtypeStruct((turns, HP, C), F32),
            ],
            input_output_aliases={11 + i: i for i in range(len(known))},
            compiler_params=params,
            cost_estimate=pl.CostEstimate(
                flops=count * 8 * 10**9, bytes_accessed=10**6, transcendentals=0
            ),
            name="payoffs",
        )(
            turn_card,
            river_at_turn,
            ranks,
            calls,
            opp_range,
            pot,
            disjoint,
            holds,
            out_of,
            tperm,
            cards,
            *known,
        )

    with jax.named_scope("payoffs"):
        delta, bet = payoffs(0, turns)
    with jax.named_scope("strategies"):
        plane, delta = lax.optimization_barrier((plane, delta))
        up, down = shifted(plane, "x", 1), shifted(plane, "x", 3)

    with jax.named_scope("river_sums"):
        mine, theirs = pl.pallas_call(
            sum_kernel,
            grid_spec=pltpu.PrefetchScalarGridSpec(
                num_scalar_prefetch=1,
                grid=(boards,),
                in_specs=[per_turn((HP, C))],
                out_specs=[whole((4, owners * owned, C))] * 2,
                scratch_shapes=[pltpu.VMEM((buckets, C), F32)] * TABLES,
            ),
            out_shape=[jax.ShapeDtypeStruct((4, owners * owned, C), F32)] * 2,
            compiler_params=params,
            cost_estimate=pl.CostEstimate(
                flops=22 * 10**9, bytes_accessed=10**6, transcendentals=0
            ),
            name="sums",
        )(index, delta)
        up, down, theirs = lax.optimization_barrier((up, down, theirs))
        got = lax.ppermute(theirs, "core", swap)
        onward = [(2 * i, (2 * i + 2) % 8) for i in range(4)]
        onward += [(2 * i + 1, (2 * i + 7) % 8) for i in range(4)]
        passed = jnp.where(lax.axis_index("core") == 0, up, down)
        far = lax.ppermute(passed, ("x", "core"), onward)
        chip = mine + got
        chip, far = lax.optimization_barrier((chip, far))
        columns = lax.all_to_all(chip, "x", 0, 0)
        own = [plane, up, far, down]
        pieces = own + [lax.ppermute(piece, "core", swap) for piece in own]
        delta, chip, *pieces = lax.optimization_barrier((delta, chip, *pieces))

    with jax.named_scope("replies"):
        replies, held, lent = pl.pallas_call(
            functools.partial(reply_kernel, turns, rivers, river_total, len(pieces)),
            grid_spec=pltpu.PrefetchScalarGridSpec(
                num_scalar_prefetch=4,
                grid=(turns,),
                in_specs=[
                    per_turn((rivers, H)),
                    whole((turns, H)),
                    per_board((HP, C)),
                    per_turn((HP, C)),
                    whole((G, H)),
                    whole((1, G)),
                    whole((HP, HP)),
                    whole((64, HP)),
                    whole((HP, 256)),
                    whole((8, HP)),
                ]
                + [pl.BlockSpec(memory_space=pl.ANY)] * len(pieces),
                out_specs=[
                    whole((owners, sent_rows, 128)),
                    whole((4, owners * towned // 2, C)),
                    whole((4, owners * towned // 2, C)),
                ],
                scratch_shapes=[
                    pltpu.VMEM((tbuckets // 2, C), F32),
                    pltpu.VMEM((rest * devices, C), F32),
                    pltpu.VMEM((2, rivers + 1, HP, C), F32),
                    pltpu.VMEM((HP, C), F32),
                    pltpu.VMEM((C, HP), F32),
                    pltpu.VMEM((8, HP), jnp.int32),
                    pltpu.VMEM((8, HP), jnp.int32),
                    pltpu.VMEM((rivers, HP, C), F32),
                    pltpu.VMEM((rivers, HP, 2 * C), BF),
                    pltpu.VMEM((rivers, 256, C), BF),
                    pltpu.VMEM((HP, C), F32),
                    pltpu.SemaphoreType.DMA((len(pieces),)),
                ],
            ),
            out_shape=[
                jax.ShapeDtypeStruct((owners, sent_rows, 128), F32),
                jax.ShapeDtypeStruct((4, owners * towned // 2, C), F32),
                jax.ShapeDtypeStruct((4, owners * towned // 2, C), F32),
            ],
            compiler_params=params,
            cost_estimate=pl.CostEstimate(
                flops=30 * 10**9, bytes_accessed=10**6, transcendentals=0
            ),
            name="replies",
        )(
            river_at,
            turn_at,
            turn_card,
            river_at_turn,
            ranks,
            turn_bucket,
            delta,
            bet,
            player_range,
            pot,
            disjoint,
            holds,
            out_of,
            cards,
            *pieces,
        )
    with jax.named_scope("turn_sums"):
        held = held + lax.ppermute(lent, "core", swap)
        turn_parts = [held[0]] + [shifted(held[s], "x", s) for s in (2, 1, 3)]

    with jax.named_scope("exchange"):
        replies, columns, turn_parts = lax.optimization_barrier((replies, columns, turn_parts))
        turn_sums, column = sum(turn_parts[1:], turn_parts[0]), columns.sum(0)
        sent = replies.at[:, turn_row:river_row].set(turn_sums.reshape(owners, -1, 128))
        sent = sent.at[:, river_row:].set(column.reshape(owners, -1, 128))
        came = lax.all_to_all(sent, ("z", "y"), 0, 0)

    with jax.named_scope("update"):
        new_river, new_turn, br_value = pl.pallas_call(
            functools.partial(update_kernel, 1.0 / river_total, each),
            out_shape=[
                jax.ShapeDtypeStruct(river_regret.shape, F32),
                jax.ShapeDtypeStruct(turn_regret.shape, F32),
                jax.ShapeDtypeStruct((turns, each, H), F32),
            ],
            compiler_params=params,
            name="update",
        )(came, river_regret, turn_regret, rperm, tperm)
    return new_river, new_turn, br_value


def solution(mesh):
    mesh = Mesh(mesh.devices.reshape(4, 2, 4, 4), AXES)
    turn, river = AXES[:2], AXES[2:]
    placed = (
        P(AXES, None),
        P(AXES, None),
        P(turn, river, None),
        P(turn, None),
        P(turn, river, None),
        P(turn),
        P(turn, river),
        P(),
        P(),
        P(turn, river, None, None),
        P(),
    )
    return jax.shard_map(
        per_device,
        mesh=mesh,
        in_specs=placed,
        out_specs=(P(AXES, None), P(AXES, None), P(turn, river, None)),
        check_vma=False,
    )
```

```python
import functools

import jax
import jax.numpy as jnp
import ml_dtypes
import numpy as np
from jax import lax
from jax.experimental import pallas as pl
from jax.experimental.pallas import tpu as pltpu
from jax.sharding import Mesh
from jax.sharding import PartitionSpec as P

CARDS = 47
H = CARDS * (CARDS - 1) // 2
HP = 1152
G = 64
C = 2 * G
BF = jnp.bfloat16
F32 = jnp.float32
NT = (((1,), (1,)), ((), ()))
NN = (((1,), (0,)), ((), ()))
TABLES = 6
UNROLL = 47
INDEX_ROW = 2048
RANKS = 16384.0
AXES = ("x", "core", "z", "y")
VMEM_LIMIT = 60 * 1024 * 1024


def constants():
    first, second = np.triu_indices(CARDS, 1)
    share = (
        (first[:, None] == first[None, :])
        | (first[:, None] == second[None, :])
        | (second[:, None] == first[None, :])
        | (second[:, None] == second[None, :])
    )
    disjoint = np.zeros((HP, HP), np.float32)
    disjoint[:H, :H] = ~share
    cards = np.full((8, HP), -1, np.int32)
    cards[0, :H] = first
    cards[1, :H] = second
    holds = np.zeros((64, HP), np.float32)
    holds[first, np.arange(H)] = 1
    holds[second, np.arange(H)] = 1
    holds[CARDS, :H] = 1
    spread_out = np.zeros((HP, 64), np.float32)
    spread_out[:H, :CARDS] = -holds[:CARDS, :H].T
    spread_out[:H, CARDS] = 1
    spread_out = np.concatenate([spread_out] * 3 + [np.zeros_like(spread_out)], axis=1)
    river_perm = np.zeros((4 * G, 4 * G), np.float32)
    turn_perm = np.zeros((2 * G, 2 * G), np.float32)
    for g in range(G):
        for a in range(2):
            turn_perm[g * 2 + a, a * G + g] = 1
            for b in range(2):
                river_perm[g * 4 + a * 2 + b, b * C + a * G + g] = 1
    halves = [m.astype(ml_dtypes.bfloat16) for m in (disjoint, holds, spread_out, river_perm, turn_perm)]
    return halves + [cards]


def others(x, holds_ref, out_of_ref):
    sums = lax.dot_general(holds_ref[...], x, NN, preferred_element_type=F32)
    pieces = parts(sums, 3)
    pieces = jnp.concatenate(pieces + [jnp.zeros_like(pieces[0])], axis=0)
    return x.astype(F32) + lax.dot_general(
        out_of_ref[...], pieces, NN, preferred_element_type=F32
    )


def parts(x, count):
    out = []
    for _ in range(count):
        piece = x.astype(BF)
        out.append(piece)
        x = x - piece.astype(F32)
    return out


def permuted(x, perm, dims):
    hi, mid, lo = [
        lax.dot_general(piece, perm, dims, preferred_element_type=F32) for piece in parts(x, 3)
    ]
    return (hi + mid) + lo


def first_share(pos0, pos1):
    total = pos0 + pos1
    some = total > 0.0
    safe = jnp.where(some, total, 1.0)
    return jnp.where(some, pos0 / safe, 0.5), jnp.where(some, pos1 / safe, 0.5)


def river_shares(permuted_regret):
    pos = jnp.maximum(permuted_regret, 0.0)
    return first_share(pos[:, :C], pos[:, C:])


def turn_shares(permuted_regret):
    pos = jnp.maximum(permuted_regret, 0.0)
    return first_share(pos, pltpu.roll(pos, G, 1))


def strategy_kernel(
    river_ref,
    turn_ref,
    rperm_ref,
    tperm_ref,
    bucket_ref,
    tbucket_ref,
    out_ref,
    index_ref,
    at_ref,
    tat_ref,
):
    owned, towned = river_ref.shape[0], turn_ref.shape[0]
    rest = owned + towned
    share, _ = river_shares(permuted(river_ref[...], rperm_ref[...], NN))
    tshare, _ = turn_shares(permuted(turn_ref[...], tperm_ref[...], NN))
    for i in range(out_ref.shape[0]):
        out_ref[i, :owned, :] = share
        out_ref[i, owned:, :] = tshare

    turns, rivers, _ = bucket_ref.shape
    index_ref[...] = jnp.zeros_like(index_ref)
    tat_ref[...] = jnp.zeros_like(tat_ref)
    for j in range(HP // 128):
        width = min(128, H - j * 128)
        lanes = slice(j * 128, j * 128 + width)
        for t in range(turns):
            tat_ref[t, j : j + 1, :width] = tbucket_ref[t : t + 1, lanes]
            for r in range(rivers):
                index_ref[t * rivers + r, j : j + 1, :width] = bucket_ref[t, r : r + 1, lanes]

    x, core = lax.axis_index("x"), lax.axis_index("core")

    def placed(bucket, count, offset):
        owner = ((bucket.astype(F32) + 0.5) * (1.0 / count)).astype(jnp.int32)
        row = bucket - owner * count
        owner_core = (owner >> 4) & 1
        other = (core - owner_core) & 1
        steps = (x - (owner >> 5)) * (1 - 2 * owner_core)
        slot = (other * 4 + (steps & 3)) * 16 + (owner & 15)
        return slot * rest + offset + row

    at_ref[...] = placed(index_ref[...], owned, 0)
    tat_ref[...] = placed(tat_ref[...], towned, owned)


def update_kernel(
    scale, each, came_ref, river_ref, turn_ref, rperm_ref, tperm_ref, river_out, turn_out, br_out
):
    turns = br_out.shape[0]
    blocks = HP // 128
    came = came_ref[0]
    for source in range(1, came_ref.shape[0]):
        came = came + came_ref[source]
    for t in range(turns):
        for j in range(blocks):
            row = (t * blocks + j) * each
            width = min(128, H - j * 128)
            br_out[t, :, j * 128 : j * 128 + width] = came[row : row + each, :width]
    at = turns * blocks * each
    rsum = came[at + 4 : at + 4 + river_ref.shape[0]]
    tsum = came[at : at + 4]
    rp = permuted(river_ref[...], rperm_ref[...], NN)
    s0, s1 = river_shares(rp)
    gain = rsum * scale
    new = jnp.maximum(rp + jnp.concatenate([s1 * gain, -(s0 * gain)], axis=1), 0.0)
    river_out[...] = permuted(new, rperm_ref[...], NT)
    tp = permuted(turn_ref[...], tperm_ref[...], NN)
    _, other = turn_shares(tp)
    lane = lax.broadcasted_iota(jnp.int32, tsum.shape, 1)
    swapped = pltpu.roll(tsum, G, 1)
    low = jnp.where(lane < G, tsum, -swapped)
    high = jnp.where(lane < G, swapped, -tsum)
    gain = jnp.concatenate([low, high], axis=0) * scale
    turn_out[...] = permuted(jnp.maximum(tp + other * gain, 0.0), tperm_ref[...], NT)


def stake_rows(pot_ref):
    pot = pot_ref[...]
    lane = lax.broadcasted_iota(jnp.int32, (1, C), 1)
    bet = 0.5 * jnp.concatenate([pot, pot], axis=1) + jnp.where(lane >= G, 2.0, 0.0)
    return bet * (1.0 / H), (bet + 2.0) * (1.0 / H)


def playable(first, second, turn_value, river_value):
    return (
        (first != turn_value)
        & (second != turn_value)
        & (first != river_value)
        & (second != river_value)
    )


def for_each_hand(index_ref, board, body):
    base = board * INDEX_ROW

    def some(i, _):
        for j in range(UNROLL):
            h = i * UNROLL + j
            body(h, index_ref[base + h], j)
        return 0

    lax.fori_loop(0, H // UNROLL, some, 0)


def widen(wide_s, narrow_ref, out_s):
    wide_s[...] = jnp.zeros_like(wide_s)
    wide_s[:G, :H] = narrow_ref[...]
    wide_s[G:, :H] = narrow_ref[...]
    out_s[...] = jnp.transpose(wide_s[...])


def sign_matrix(rank_ref, r, turn_value, river_value, cards_ref, disjoint_ref, rank_s):
    out = jnp.logical_not(
        playable(cards_ref[0:1, :], cards_ref[1:2, :], turn_value, river_value)
    )
    rank_s[r : r + 1, :H] = rank_ref[0, r : r + 1, :]
    rank_row = rank_s[r : r + 1, :].astype(F32) + jnp.where(out, RANKS, 0.0)
    rank_col = jnp.transpose(jnp.broadcast_to(rank_row, (128, HP)))
    signed = []
    for j in range(HP // 128):
        lanes = slice(j * 128, (j + 1) * 128)
        more = (rank_col - rank_row[:, lanes]).astype(BF)
        bound = disjoint_ref[:, lanes]
        signed.append(jnp.maximum(jnp.minimum(more, bound), -bound))
    return rank_col < RANKS, jnp.concatenate(signed, axis=1)


def payoff_kernel(
    rivers,
    start,
    tcard_ref,
    rcard_ref,
    rank_ref,
    call_ref,
    opp_ref,
    pot_ref,
    disjoint_ref,
    holds_ref,
    out_of_ref,
    tperm_ref,
    cards_ref,
    *refs,
):
    (
        delta_ref,
        bet_ref,
        rank_s,
        call_s,
        wide_s,
        opp_s,
        show_s,
    ) = refs[-7:]
    t = pl.program_id(0) + start

    @pl.when(t == start)
    def _():
        rank_s[...] = jnp.zeros_like(rank_s)
        call_s[rivers * H :, :] = jnp.zeros((rivers * (HP - H), C), F32)
        widen(wide_s, opp_ref, opp_s)

    call_s[: rivers * H, :] = lax.dot_general(
        call_ref[0].reshape(rivers * H, C), tperm_ref[...], NN, preferred_element_type=F32
    )
    low, high = stake_rows(pot_ref)
    bets = 0.0
    for r in range(rivers):
        col_ok, signed = sign_matrix(
            rank_ref, r, tcard_ref[t], rcard_ref[r, t], cards_ref, disjoint_ref, rank_s
        )
        called = call_s[pl.ds(r, HP, stride=rivers), :]
        theirs = jnp.where(col_ok, opp_s[...], 0.0)
        show_s[r, :, :C] = theirs.astype(BF)
        show_s[r, :, C:] = (theirs * called).astype(BF)
        show = lax.dot_general(signed, show_s[r], NN, preferred_element_type=F32)
        fold = others((theirs * (1.0 - called)).astype(BF), holds_ref, out_of_ref)
        bet = jnp.where(col_ok, high * show[:, C:] + low * fold, 0.0)
        delta_ref[r] = jnp.where(col_ok, low * show[:, :C], 0.0) - bet
        bets = bets + bet
    bet_ref[0] = bets


def sum_kernel(index_ref, delta_ref, mine_ref, theirs_ref, *tables):
    board = pl.program_id(0)

    @pl.when(board == 0)
    def _():
        for table in tables:
            table[...] = jnp.zeros_like(table)

    def add_row(h, k, j):
        table = tables[j % TABLES]
        table[pl.ds(k, 1), :] += delta_ref[0, pl.ds(h, 1), :]

    for_each_hand(index_ref, board, add_row)

    @pl.when(board == pl.num_programs(0) - 1)
    def _():
        core = lax.axis_index("core")
        rows = mine_ref.shape[1]
        for s in range(mine_ref.shape[0]):
            for out_ref, c in ((mine_ref, core), (theirs_ref, 1 - core)):
                at = pl.multiple_of((s * 2 + c) * rows, 8)
                total = tables[0][pl.ds(at, rows), :]
                for table in tables[1:]:
                    total = total + table[pl.ds(at, rows), :]
                out_ref[s] = total


def reply_kernel(
    turns,
    rivers,
    river_total,
    pieces,
    bucket_ref,
    tbucket_ref,
    tcard_ref,
    rcard_ref,
    rank_ref,
    trow_ref,
    delta_ref,
    bet_ref,
    mine_ref,
    pot_ref,
    disjoint_ref,
    holds_ref,
    out_of_ref,
    cards_ref,
    *refs,
):
    piece_refs = refs[:pieces]
    (
        out_ref,
        held_ref,
        lent_ref,
        gain_ref,
        table_s,
        rows_s,
        mine_s,
        wide_s,
        rank_s,
        trow_s,
        col_s,
        reach_s,
        sums_s,
        reply_s,
        sem,
    ) = refs[pieces:]
    t = pl.program_id(0)
    now, later = t % 2, (t + 1) % 2
    kinds = rivers + 1

    def take_rows(first, count, turn, slot):
        for j in range(count):
            h = first + j
            k = tbucket_ref[turn * INDEX_ROW + h]
            rows_s[slot, 0, pl.ds(h, 1), :] = table_s[pl.ds(k, 1), :]
            for r in range(rivers):
                k = bucket_ref[(turn * rivers + r) * INDEX_ROW + h]
                rows_s[slot, r + 1, pl.ds(h, 1), :] = table_s[pl.ds(k, 1), :]

    @pl.when(t == 0)
    def _():
        at, copies = 0, []
        for i, piece in enumerate(piece_refs):
            rows = piece.shape[0]
            copies.append(pltpu.make_async_copy(piece, table_s.at[pl.ds(at, rows)], sem.at[i]))
            copies[-1].start()
            at += rows
        rank_s[...] = jnp.zeros_like(rank_s)
        trow_s[...] = jnp.full_like(trow_s, -1)
        gain_ref[...] = jnp.zeros_like(gain_ref)
        widen(wide_s, mine_ref, mine_s)
        for slot in range(2):
            for kind in range(kinds):
                rows_s[slot, kind, H:, :] = jnp.zeros((HP - H, C), F32)
        for copy in copies:
            copy.wait()

        def some(i, _):
            take_rows(i * UNROLL, UNROLL, 0, 0)
            return 0

        lax.fori_loop(0, H // UNROLL, some, 0)

    low, high = stake_rows(pot_ref)
    reach = mine_s[...] * rows_s[now, 0]
    nodes = bet_ref[0]
    for r in range(rivers):
        first = rows_s[now, r + 1]
        out = jnp.logical_not(
            playable(cards_ref[0:1, :], cards_ref[1:2, :], tcard_ref[t], rcard_ref[r, t])
        )
        rank_s[r : r + 1, :H] = rank_ref[0, r : r + 1, :]
        rank_row = rank_s[r : r + 1, :].astype(F32) + jnp.where(out, RANKS, 0.0)
        col_s[r] = jnp.transpose(jnp.broadcast_to(rank_row, (128, HP)))
        col_ok = col_s[r] < RANKS
        reach_s[r, :, :C] = jnp.where(col_ok, reach * first, 0.0).astype(BF)
        reach_s[r, :, C:] = jnp.where(col_ok, reach * (1.0 - first), 0.0).astype(BF)
        sums = lax.dot_general(
            holds_ref[...], reach_s[r, :, C:], NN, preferred_element_type=F32
        )
        split = parts(sums, 3)
        sums_s[r] = jnp.concatenate(split + [jnp.zeros_like(split[0])], axis=0)
        nodes = nodes + first * delta_ref[r]
    rank_rows = [
        rank_s[r : r + 1, :].astype(F32)
        + jnp.where(
            playable(cards_ref[0:1, :], cards_ref[1:2, :], tcard_ref[t], rcard_ref[r, t]),
            0.0,
            RANKS,
        )
        for r in range(rivers)
    ]

    def some_replies(at, count):
        rows = pl.ds(at, count)
        total = 0.0
        for r in range(rivers):
            col = col_s[r, rows, :]
            signed = []
            for j in range(HP // 128):
                lanes = slice(j * 128, (j + 1) * 128)
                more = (col - rank_rows[r][:, lanes]).astype(BF)
                bound = disjoint_ref[rows, lanes]
                signed.append(jnp.maximum(jnp.minimum(more, bound), -bound))
            against = lax.dot_general(
                jnp.concatenate(signed, axis=1), reach_s[r], NN, preferred_element_type=F32
            )
            against_bet = reach_s[r, rows, C:].astype(F32) + lax.dot_general(
                out_of_ref[rows, :], sums_s[r], NN, preferred_element_type=F32
            )
            reply = low * against[:, :C] + jnp.maximum(
                high * against[:, C:], -(low * against_bet)
            )
            total = total + jnp.where(col < RANKS, reply, 0.0)
        reply_s[rows, :] = total


    some_replies(0, HP)

    hi, lo = parts(nodes - pltpu.roll(nodes, G, 1), 2)
    both = jnp.concatenate([hi[:, :G], lo[:, :G]], axis=1)
    trow_s[0:1, :H] = trow_ref[pl.ds(t, 1), :]
    trow = trow_s[0:1, :]
    row = lax.broadcasted_iota(jnp.int32, (gain_ref.shape[0], HP), 0)
    bucket = row // 4 * 8 + row % 4

    def sums_of(ids):
        hot = jnp.where(ids == trow, 1.0, 0.0).astype(BF)
        out = lax.dot_general(hot, both, NN, preferred_element_type=F32)
        return out + pltpu.roll(out, G, 1)

    lane = lax.broadcasted_iota(jnp.int32, gain_ref.shape, 1)
    gain_ref[...] += jnp.where(lane < G, sums_of(bucket), sums_of(bucket + 4))

    @pl.when(t == turns - 1)
    def _():
        x, core = lax.axis_index("x"), lax.axis_index("core")
        ring, count, _ = held_ref.shape
        for s in range(ring):
            for part_ref, c in ((held_ref, core), (lent_ref, 1 - core)):
                at = pl.multiple_of((((x + s) & 3) * 2 + c) * count, 8)
                part_ref[s] = gain_ref[pl.ds(at, count), :]

    @pl.when(t < turns - 1)
    def _():
        def some(i, _):
            take_rows(i * UNROLL, UNROLL, t + 1, later)
            return 0

        lax.fori_loop(0, H // UNROLL, some, 0)

    flat = jnp.transpose(reply_s[...])
    flat = (flat[:G] + flat[G:]) * (1.0 / river_total)
    owners = out_ref.shape[0]
    each = G // owners
    blocks = HP // 128
    for turn in range(turns):

        @pl.when(t == turn)
        def _():
            for j in range(blocks):
                piece = flat[:, j * 128 : (j + 1) * 128].reshape(owners, each, 128)
                row = (turn * blocks + j) * each
                out_ref[:, row : row + each, :] = piece


def shifted(x, axis, shift):
    return lax.ppermute(x, axis, [(i, (i + shift) % 4) for i in range(4)])


def per_device(
    river_regret,
    turn_regret,
    river_bucket,
    turn_bucket,
    ranks,
    turn_card,
    river_card,
    player_range,
    opp_range,
    call_prob,
    base_pot,
):
    turns, rivers, _ = river_bucket.shape
    boards = turns * rivers
    devices = 128
    owners = 16
    each = G // owners
    river_total = rivers * owners
    owned, towned = river_regret.shape[0], turn_regret.shape[0]
    buckets, tbuckets = owned * devices, towned * devices
    disjoint, holds, out_of, rperm, tperm, cards = constants()
    params = pltpu.CompilerParams(vmem_limit_bytes=VMEM_LIMIT)
    pot = base_pot.reshape(1, G)
    calls = jnp.transpose(call_prob, (0, 3, 1, 2))
    river_at_turn = river_card.T
    rest = owned + towned
    swap = [(0, 1), (1, 0)]
    turn_row = turns * (HP // 128) * each
    river_row = turn_row + towned // 2
    sent_rows = river_row + owned

    with jax.named_scope("strategies"):
        strategies, *indices = pl.pallas_call(
            strategy_kernel,
            out_shape=[
                jax.ShapeDtypeStruct((owners, rest, C), F32),
                jax.ShapeDtypeStruct((boards, INDEX_ROW // 128, 128), jnp.int32),
                jax.ShapeDtypeStruct((boards, INDEX_ROW // 128, 128), jnp.int32),
                jax.ShapeDtypeStruct((turns, INDEX_ROW // 128, 128), jnp.int32),
            ],
            compiler_params=params,
            name="strategies",
        )(river_regret, turn_regret, rperm, tperm, river_bucket, turn_bucket)
        index, river_at, turn_at = (a.reshape(-1) for a in indices)
        plane = lax.all_to_all(strategies, ("z", "y"), 0, 0).reshape(-1, C)

    def whole(shape):
        return pl.BlockSpec(shape, lambda i, *_: (0,) * len(shape))

    def per_turn(shape, count=1):
        return pl.BlockSpec((count,) + shape, lambda i, *_: (i,) + (0,) * len(shape))

    def per_board(shape):
        return per_turn(shape, rivers)

    def payoffs(start, count, known=()):
        def of_turn(shape, each_turn=1):
            return pl.BlockSpec(
                (each_turn,) + shape, lambda i, *_: (i + start,) + (0,) * len(shape)
            )

        return pl.pallas_call(
            functools.partial(payoff_kernel, rivers, start),
            grid_spec=pltpu.PrefetchScalarGridSpec(
                num_scalar_prefetch=2,
                grid=(count,),
                in_specs=[
                    of_turn((rivers, H)),
                    of_turn((H, rivers, C)),
                    whole((G, H)),
                    whole((1, G)),
                    whole((HP, HP)),
                    whole((64, HP)),
                    whole((HP, 256)),
                    whole((C, C)),
                    whole((8, HP)),
                ]
                + [pl.BlockSpec(memory_space=pl.ANY)] * len(known),
                out_specs=[of_turn((HP, C), rivers), of_turn((HP, C))],
                scratch_shapes=[
                    pltpu.VMEM((8, HP), jnp.int32),
                    pltpu.VMEM((rivers * HP, C), F32),
                    pltpu.VMEM((C, HP), F32),
                    pltpu.VMEM((HP, C), F32),
                    pltpu.VMEM((rivers, HP, 2 * C), BF),
                ],
            ),
            out_shape=[
                jax.ShapeDtypeStruct((boards, HP, C), F32),
                jax.ShapeDtypeStruct((turns, HP, C), F32),
            ],
            input_output_aliases={11 + i: i for i in range(len(known))},
            compiler_params=params,
            cost_estimate=pl.CostEstimate(
                flops=count * 8 * 10**9, bytes_accessed=10**6, transcendentals=0
            ),
            name="payoffs",
        )(
            turn_card,
            river_at_turn,
            ranks,
            calls,
            opp_range,
            pot,
            disjoint,
            holds,
            out_of,
            tperm,
            cards,
            *known,
        )

    with jax.named_scope("payoffs"):
        delta, bet = payoffs(0, turns)
    with jax.named_scope("strategies"):
        plane, delta = lax.optimization_barrier((plane, delta))
        onward = [(2 * i, (2 * i + 2) % 8) for i in range(4)]
        onward += [(2 * i + 1, (2 * i + 7) % 8) for i in range(4)]
        back = [(j, i) for i, j in onward]
        near = lax.ppermute(plane, ("x", "core"), onward)
        last = lax.ppermute(plane, ("x", "core"), back)

    with jax.named_scope("river_sums"):
        mine, theirs = pl.pallas_call(
            sum_kernel,
            grid_spec=pltpu.PrefetchScalarGridSpec(
                num_scalar_prefetch=1,
                grid=(boards,),
                in_specs=[per_turn((HP, C))],
                out_specs=[whole((4, owners * owned, C))] * 2,
                scratch_shapes=[pltpu.VMEM((buckets, C), F32)] * TABLES,
            ),
            out_shape=[jax.ShapeDtypeStruct((4, owners * owned, C), F32)] * 2,
            compiler_params=params,
            cost_estimate=pl.CostEstimate(
                flops=22 * 10**9, bytes_accessed=10**6, transcendentals=0
            ),
            name="sums",
        )(index, delta)
        near, last, theirs = lax.optimization_barrier((near, last, theirs))
        got = lax.ppermute(theirs, "core", swap)
        far = lax.ppermute(near, ("x", "core"), onward)
        chip = mine + got
        chip, far = lax.optimization_barrier((chip, far))
        columns = lax.all_to_all(chip, "x", 0, 0)
        own = [plane, near, far, last]
        pieces = own + [lax.ppermute(piece, "core", swap) for piece in own]
        delta, chip, *pieces = lax.optimization_barrier((delta, chip, *pieces))

    with jax.named_scope("replies"):
        replies, held, lent = pl.pallas_call(
            functools.partial(reply_kernel, turns, rivers, river_total, len(pieces)),
            grid_spec=pltpu.PrefetchScalarGridSpec(
                num_scalar_prefetch=4,
                grid=(turns,),
                in_specs=[
                    per_turn((rivers, H)),
                    whole((turns, H)),
                    per_board((HP, C)),
                    per_turn((HP, C)),
                    whole((G, H)),
                    whole((1, G)),
                    whole((HP, HP)),
                    whole((64, HP)),
                    whole((HP, 256)),
                    whole((8, HP)),
                ]
                + [pl.BlockSpec(memory_space=pl.ANY)] * len(pieces),
                out_specs=[
                    whole((owners, sent_rows, 128)),
                    whole((4, owners * towned // 2, C)),
                    whole((4, owners * towned // 2, C)),
                ],
                scratch_shapes=[
                    pltpu.VMEM((tbuckets // 2, C), F32),
                    pltpu.VMEM((rest * devices, C), F32),
                    pltpu.VMEM((2, rivers + 1, HP, C), F32),
                    pltpu.VMEM((HP, C), F32),
                    pltpu.VMEM((C, HP), F32),
                    pltpu.VMEM((8, HP), jnp.int32),
                    pltpu.VMEM((8, HP), jnp.int32),
                    pltpu.VMEM((rivers, HP, C), F32),
                    pltpu.VMEM((rivers, HP, 2 * C), BF),
                    pltpu.VMEM((rivers, 256, C), BF),
                    pltpu.VMEM((HP, C), F32),
                    pltpu.SemaphoreType.DMA((len(pieces),)),
                ],
            ),
            out_shape=[
                jax.ShapeDtypeStruct((owners, sent_rows, 128), F32),
                jax.ShapeDtypeStruct((4, owners * towned // 2, C), F32),
                jax.ShapeDtypeStruct((4, owners * towned // 2, C), F32),
            ],
            compiler_params=params,
            cost_estimate=pl.CostEstimate(
                flops=30 * 10**9, bytes_accessed=10**6, transcendentals=0
            ),
            name="replies",
        )(
            river_at,
            turn_at,
            turn_card,
            river_at_turn,
            ranks,
            turn_bucket,
            delta,
            bet,
            player_range,
            pot,
            disjoint,
            holds,
            out_of,
            cards,
            *pieces,
        )
    with jax.named_scope("turn_sums"):
        held = held + lax.ppermute(lent, "core", swap)
        turn_parts = [held[0]] + [shifted(held[s], "x", s) for s in (2, 1, 3)]

    with jax.named_scope("exchange"):
        replies, columns, turn_parts = lax.optimization_barrier((replies, columns, turn_parts))
        turn_sums, column = sum(turn_parts[1:], turn_parts[0]), columns.sum(0)
        sent = replies.at[:, turn_row:river_row].set(turn_sums.reshape(owners, -1, 128))
        sent = sent.at[:, river_row:].set(column.reshape(owners, -1, 128))
        came = lax.all_to_all(sent, ("z", "y"), 0, 0)

    with jax.named_scope("update"):
        new_river, new_turn, br_value = pl.pallas_call(
            functools.partial(update_kernel, 1.0 / river_total, each),
            out_shape=[
                jax.ShapeDtypeStruct(river_regret.shape, F32),
                jax.ShapeDtypeStruct(turn_regret.shape, F32),
                jax.ShapeDtypeStruct((turns, each, H), F32),
            ],
            compiler_params=params,
            name="update",
        )(came, river_regret, turn_regret, rperm, tperm)
    return new_river, new_turn, br_value


def solution(mesh):
    mesh = Mesh(mesh.devices.reshape(4, 2, 4, 4), AXES)
    turn, river = AXES[:2], AXES[2:]
    placed = (
        P(AXES, None),
        P(AXES, None),
        P(turn, river, None),
        P(turn, None),
        P(turn, river, None),
        P(turn),
        P(turn, river),
        P(),
        P(),
        P(turn, river, None, None),
        P(),
    )
    return jax.shard_map(
        per_device,
        mesh=mesh,
        in_specs=placed,
        out_specs=(P(AXES, None), P(AXES, None), P(turn, river, None)),
        check_vma=False,
    )
```

```python
import functools

import jax
import jax.numpy as jnp
import ml_dtypes
import numpy as np
from jax import lax
from jax.experimental import pallas as pl
from jax.experimental.pallas import tpu as pltpu
from jax.sharding import Mesh
from jax.sharding import PartitionSpec as P

CARDS = 47
H = CARDS * (CARDS - 1) // 2
HP = 1152
G = 64
C = 2 * G
BF = jnp.bfloat16
F32 = jnp.float32
NT = (((1,), (1,)), ((), ()))
NN = (((1,), (0,)), ((), ()))
TABLES = 6
UNROLL = 47
INDEX_ROW = 2048
RANKS = 16384.0
AXES = ("x", "core", "z", "y")
VMEM_LIMIT = 44 * 1024 * 1024


def constants():
    first, second = np.triu_indices(CARDS, 1)
    share = (
        (first[:, None] == first[None, :])
        | (first[:, None] == second[None, :])
        | (second[:, None] == first[None, :])
        | (second[:, None] == second[None, :])
    )
    disjoint = np.zeros((HP, HP), np.float32)
    disjoint[:H, :H] = ~share
    cards = np.full((8, HP), -1, np.int32)
    cards[0, :H] = first
    cards[1, :H] = second
    holds = np.zeros((64, HP), np.float32)
    holds[first, np.arange(H)] = 1
    holds[second, np.arange(H)] = 1
    holds[CARDS, :H] = 1
    spread_out = np.zeros((HP, 64), np.float32)
    spread_out[:H, :CARDS] = -holds[:CARDS, :H].T
    spread_out[:H, CARDS] = 1
    spread_out = np.concatenate([spread_out] * 3 + [np.zeros_like(spread_out)], axis=1)
    river_perm = np.zeros((4 * G, 4 * G), np.float32)
    turn_perm = np.zeros((2 * G, 2 * G), np.float32)
    for g in range(G):
        for a in range(2):
            turn_perm[g * 2 + a, a * G + g] = 1
            for b in range(2):
                river_perm[g * 4 + a * 2 + b, b * C + a * G + g] = 1
    halves = [m.astype(ml_dtypes.bfloat16) for m in (disjoint, holds, spread_out, river_perm, turn_perm)]
    return halves + [cards]


def others(x, holds_ref, out_of_ref):
    sums = lax.dot_general(holds_ref[...], x, NN, preferred_element_type=F32)
    pieces = parts(sums, 3)
    pieces = jnp.concatenate(pieces + [jnp.zeros_like(pieces[0])], axis=0)
    return x.astype(F32) + lax.dot_general(
        out_of_ref[...], pieces, NN, preferred_element_type=F32
    )


def parts(x, count):
    out = []
    for _ in range(count):
        piece = x.astype(BF)
        out.append(piece)
        x = x - piece.astype(F32)
    return out


def permuted(x, perm, dims):
    hi, mid, lo = [
        lax.dot_general(piece, perm, dims, preferred_element_type=F32) for piece in parts(x, 3)
    ]
    return (hi + mid) + lo


def first_share(pos0, pos1):
    total = pos0 + pos1
    some = total > 0.0
    safe = jnp.where(some, total, 1.0)
    return jnp.where(some, pos0 / safe, 0.5), jnp.where(some, pos1 / safe, 0.5)


def river_shares(permuted_regret):
    pos = jnp.maximum(permuted_regret, 0.0)
    return first_share(pos[:, :C], pos[:, C:])


def turn_shares(permuted_regret):
    pos = jnp.maximum(permuted_regret, 0.0)
    return first_share(pos, pltpu.roll(pos, G, 1))


def strategy_kernel(
    river_ref,
    turn_ref,
    rperm_ref,
    tperm_ref,
    bucket_ref,
    tbucket_ref,
    out_ref,
    index_ref,
    at_ref,
    tat_ref,
):
    owned, towned = river_ref.shape[0], turn_ref.shape[0]
    rest = owned + towned
    share, _ = river_shares(permuted(river_ref[...], rperm_ref[...], NN))
    tshare, _ = turn_shares(permuted(turn_ref[...], tperm_ref[...], NN))
    for i in range(out_ref.shape[0]):
        out_ref[i, :owned, :] = share
        out_ref[i, owned:, :] = tshare

    turns, rivers, _ = bucket_ref.shape
    index_ref[...] = jnp.zeros_like(index_ref)
    tat_ref[...] = jnp.zeros_like(tat_ref)
    for j in range(HP // 128):
        width = min(128, H - j * 128)
        lanes = slice(j * 128, j * 128 + width)
        for t in range(turns):
            tat_ref[t, j : j + 1, :width] = tbucket_ref[t : t + 1, lanes]
            for r in range(rivers):
                index_ref[t * rivers + r, j : j + 1, :width] = bucket_ref[t, r : r + 1, lanes]

    x, core = lax.axis_index("x"), lax.axis_index("core")

    def placed(bucket, count, offset):
        owner = ((bucket.astype(F32) + 0.5) * (1.0 / count)).astype(jnp.int32)
        row = bucket - owner * count
        owner_core = (owner >> 4) & 1
        other = (core - owner_core) & 1
        steps = (x - (owner >> 5)) * (1 - 2 * owner_core)
        slot = (other * 4 + (steps & 3)) * 16 + (owner & 15)
        return slot * rest + offset + row

    at_ref[...] = placed(index_ref[...], owned, 0)
    tat_ref[...] = placed(tat_ref[...], towned, owned)


def update_kernel(
    scale, each, came_ref, river_ref, turn_ref, rperm_ref, tperm_ref, river_out, turn_out, br_out
):
    turns = br_out.shape[0]
    blocks = HP // 128
    came = came_ref[0]
    for source in range(1, came_ref.shape[0]):
        came = came + came_ref[source]
    for t in range(turns):
        for j in range(blocks):
            row = (t * blocks + j) * each
            width = min(128, H - j * 128)
            br_out[t, :, j * 128 : j * 128 + width] = came[row : row + each, :width]
    at = turns * blocks * each
    rsum = came[at + 4 : at + 4 + river_ref.shape[0]]
    tsum = came[at : at + 4]
    rp = permuted(river_ref[...], rperm_ref[...], NN)
    s0, s1 = river_shares(rp)
    gain = rsum * scale
    new = jnp.maximum(rp + jnp.concatenate([s1 * gain, -(s0 * gain)], axis=1), 0.0)
    river_out[...] = permuted(new, rperm_ref[...], NT)
    tp = permuted(turn_ref[...], tperm_ref[...], NN)
    _, other = turn_shares(tp)
    lane = lax.broadcasted_iota(jnp.int32, tsum.shape, 1)
    swapped = pltpu.roll(tsum, G, 1)
    low = jnp.where(lane < G, tsum, -swapped)
    high = jnp.where(lane < G, swapped, -tsum)
    gain = jnp.concatenate([low, high], axis=0) * scale
    turn_out[...] = permuted(jnp.maximum(tp + other * gain, 0.0), tperm_ref[...], NT)


def stake_rows(pot_ref):
    pot = pot_ref[...]
    lane = lax.broadcasted_iota(jnp.int32, (1, C), 1)
    bet = 0.5 * jnp.concatenate([pot, pot], axis=1) + jnp.where(lane >= G, 2.0, 0.0)
    return bet * (1.0 / H), (bet + 2.0) * (1.0 / H)


def playable(first, second, turn_value, river_value):
    return (
        (first != turn_value)
        & (second != turn_value)
        & (first != river_value)
        & (second != river_value)
    )


def for_each_hand(index_ref, board, body):
    base = board * INDEX_ROW

    def some(i, _):
        for j in range(UNROLL):
            h = i * UNROLL + j
            body(h, index_ref[base + h], j)
        return 0

    lax.fori_loop(0, H // UNROLL, some, 0)


def widen(wide_s, narrow_ref, out_s):
    wide_s[...] = jnp.zeros_like(wide_s)
    wide_s[:G, :H] = narrow_ref[...]
    wide_s[G:, :H] = narrow_ref[...]
    out_s[...] = jnp.transpose(wide_s[...])


def sign_matrix(rank_ref, r, turn_value, river_value, cards_ref, disjoint_ref, rank_s):
    out = jnp.logical_not(
        playable(cards_ref[0:1, :], cards_ref[1:2, :], turn_value, river_value)
    )
    rank_s[r : r + 1, :H] = rank_ref[0, r : r + 1, :]
    rank_row = rank_s[r : r + 1, :].astype(F32) + jnp.where(out, RANKS, 0.0)
    rank_col = jnp.transpose(jnp.broadcast_to(rank_row, (128, HP)))
    signed = []
    for j in range(HP // 128):
        lanes = slice(j * 128, (j + 1) * 128)
        more = (rank_col - rank_row[:, lanes]).astype(BF)
        bound = disjoint_ref[:, lanes]
        signed.append(jnp.maximum(jnp.minimum(more, bound), -bound))
    return rank_col < RANKS, jnp.concatenate(signed, axis=1)


def payoff_kernel(
    rivers,
    start,
    tcard_ref,
    rcard_ref,
    rank_ref,
    call_ref,
    opp_ref,
    pot_ref,
    disjoint_ref,
    holds_ref,
    out_of_ref,
    tperm_ref,
    cards_ref,
    *refs,
):
    (
        delta_ref,
        bet_ref,
        rank_s,
        call_s,
        wide_s,
        opp_s,
        show_s,
    ) = refs[-7:]
    t = pl.program_id(0) + start

    @pl.when(t == start)
    def _():
        rank_s[...] = jnp.zeros_like(rank_s)
        call_s[rivers * H :, :] = jnp.zeros((rivers * (HP - H), C), F32)
        widen(wide_s, opp_ref, opp_s)

    call_s[: rivers * H, :] = lax.dot_general(
        call_ref[0].reshape(rivers * H, C), tperm_ref[...], NN, preferred_element_type=F32
    )
    low, high = stake_rows(pot_ref)
    bets = 0.0
    for r in range(rivers):
        col_ok, signed = sign_matrix(
            rank_ref, r, tcard_ref[t], rcard_ref[r, t], cards_ref, disjoint_ref, rank_s
        )
        called = call_s[pl.ds(r, HP, stride=rivers), :]
        theirs = jnp.where(col_ok, opp_s[...], 0.0)
        show_s[r, :, :C] = theirs.astype(BF)
        show_s[r, :, C:] = (theirs * called).astype(BF)
        show = lax.dot_general(signed, show_s[r], NN, preferred_element_type=F32)
        fold = others((theirs * (1.0 - called)).astype(BF), holds_ref, out_of_ref)
        bet = jnp.where(col_ok, high * show[:, C:] + low * fold, 0.0)
        delta_ref[r] = jnp.where(col_ok, low * show[:, :C], 0.0) - bet
        bets = bets + bet
    bet_ref[0] = bets


def sum_kernel(index_ref, delta_ref, mine_ref, theirs_ref, *tables):
    board = pl.program_id(0)

    @pl.when(board == 0)
    def _():
        for table in tables:
            table[...] = jnp.zeros_like(table)

    def add_row(h, k, j):
        table = tables[j % TABLES]
        table[pl.ds(k, 1), :] += delta_ref[0, pl.ds(h, 1), :]

    for_each_hand(index_ref, board, add_row)

    @pl.when(board == pl.num_programs(0) - 1)
    def _():
        core = lax.axis_index("core")
        rows = mine_ref.shape[1]
        for s in range(mine_ref.shape[0]):
            for out_ref, c in ((mine_ref, core), (theirs_ref, 1 - core)):
                at = pl.multiple_of((s * 2 + c) * rows, 8)
                total = tables[0][pl.ds(at, rows), :]
                for table in tables[1:]:
                    total = total + table[pl.ds(at, rows), :]
                out_ref[s] = total


def reply_kernel(
    turns,
    rivers,
    river_total,
    pieces,
    bucket_ref,
    tbucket_ref,
    tcard_ref,
    rcard_ref,
    rank_ref,
    trow_ref,
    delta_ref,
    bet_ref,
    mine_ref,
    pot_ref,
    disjoint_ref,
    holds_ref,
    out_of_ref,
    cards_ref,
    *refs,
):
    piece_refs = refs[:pieces]
    (
        out_ref,
        held_ref,
        lent_ref,
        gain_ref,
        table_s,
        rows_s,
        mine_s,
        wide_s,
        rank_s,
        trow_s,
        col_s,
        reach_s,
        sums_s,
        reply_s,
        sem,
    ) = refs[pieces:]
    t = pl.program_id(0)
    now, later = t % 2, (t + 1) % 2
    kinds = rivers + 1

    def take_rows(first, count, turn, slot):
        for j in range(count):
            h = first + j
            k = tbucket_ref[turn * INDEX_ROW + h]
            rows_s[slot, 0, pl.ds(h, 1), :] = table_s[pl.ds(k, 1), :]
            for r in range(rivers):
                k = bucket_ref[(turn * rivers + r) * INDEX_ROW + h]
                rows_s[slot, r + 1, pl.ds(h, 1), :] = table_s[pl.ds(k, 1), :]

    @pl.when(t == 0)
    def _():
        at, copies = 0, []
        for i, piece in enumerate(piece_refs):
            rows = piece.shape[0]
            copies.append(pltpu.make_async_copy(piece, table_s.at[pl.ds(at, rows)], sem.at[i]))
            copies[-1].start()
            at += rows
        rank_s[...] = jnp.zeros_like(rank_s)
        trow_s[...] = jnp.full_like(trow_s, -1)
        gain_ref[...] = jnp.zeros_like(gain_ref)
        widen(wide_s, mine_ref, mine_s)
        for slot in range(2):
            for kind in range(kinds):
                rows_s[slot, kind, H:, :] = jnp.zeros((HP - H, C), F32)
        for copy in copies:
            copy.wait()

        def some(i, _):
            take_rows(i * UNROLL, UNROLL, 0, 0)
            return 0

        lax.fori_loop(0, H // UNROLL, some, 0)

    low, high = stake_rows(pot_ref)
    reach = mine_s[...] * rows_s[now, 0]
    nodes = bet_ref[0]
    for r in range(rivers):
        first = rows_s[now, r + 1]
        out = jnp.logical_not(
            playable(cards_ref[0:1, :], cards_ref[1:2, :], tcard_ref[t], rcard_ref[r, t])
        )
        rank_s[r : r + 1, :H] = rank_ref[0, r : r + 1, :]
        rank_row = rank_s[r : r + 1, :].astype(F32) + jnp.where(out, RANKS, 0.0)
        col_s[r] = jnp.transpose(jnp.broadcast_to(rank_row, (128, HP)))
        col_ok = col_s[r] < RANKS
        reach_s[r, :, :C] = jnp.where(col_ok, reach * first, 0.0).astype(BF)
        reach_s[r, :, C:] = jnp.where(col_ok, reach * (1.0 - first), 0.0).astype(BF)
        sums = lax.dot_general(
            holds_ref[...], reach_s[r, :, C:], NN, preferred_element_type=F32
        )
        split = parts(sums, 3)
        sums_s[r] = jnp.concatenate(split + [jnp.zeros_like(split[0])], axis=0)
        nodes = nodes + first * delta_ref[r]
    rank_rows = [
        rank_s[r : r + 1, :].astype(F32)
        + jnp.where(
            playable(cards_ref[0:1, :], cards_ref[1:2, :], tcard_ref[t], rcard_ref[r, t]),
            0.0,
            RANKS,
        )
        for r in range(rivers)
    ]

    def some_replies(at, count):
        rows = pl.ds(at, count)
        total = 0.0
        for r in range(rivers):
            col = col_s[r, rows, :]
            signed = []
            for j in range(HP // 128):
                lanes = slice(j * 128, (j + 1) * 128)
                more = (col - rank_rows[r][:, lanes]).astype(BF)
                bound = disjoint_ref[rows, lanes]
                signed.append(jnp.maximum(jnp.minimum(more, bound), -bound))
            against = lax.dot_general(
                jnp.concatenate(signed, axis=1), reach_s[r], NN, preferred_element_type=F32
            )
            against_bet = reach_s[r, rows, C:].astype(F32) + lax.dot_general(
                out_of_ref[rows, :], sums_s[r], NN, preferred_element_type=F32
            )
            reply = low * against[:, :C] + jnp.maximum(
                high * against[:, C:], -(low * against_bet)
            )
            total = total + jnp.where(col < RANKS, reply, 0.0)
        reply_s[rows, :] = total


    some_replies(0, HP)

    hi, lo = parts(nodes - pltpu.roll(nodes, G, 1), 2)
    both = jnp.concatenate([hi[:, :G], lo[:, :G]], axis=1)
    trow_s[0:1, :H] = trow_ref[pl.ds(t, 1), :]
    trow = trow_s[0:1, :]
    row = lax.broadcasted_iota(jnp.int32, (gain_ref.shape[0], HP), 0)
    bucket = row // 4 * 8 + row % 4

    def sums_of(ids):
        hot = jnp.where(ids == trow, 1.0, 0.0).astype(BF)
        out = lax.dot_general(hot, both, NN, preferred_element_type=F32)
        return out + pltpu.roll(out, G, 1)

    lane = lax.broadcasted_iota(jnp.int32, gain_ref.shape, 1)
    gain_ref[...] += jnp.where(lane < G, sums_of(bucket), sums_of(bucket + 4))

    @pl.when(t == turns - 1)
    def _():
        x, core = lax.axis_index("x"), lax.axis_index("core")
        ring, count, _ = held_ref.shape
        for s in range(ring):
            for part_ref, c in ((held_ref, core), (lent_ref, 1 - core)):
                at = pl.multiple_of((((x + s) & 3) * 2 + c) * count, 8)
                part_ref[s] = gain_ref[pl.ds(at, count), :]

    @pl.when(t < turns - 1)
    def _():
        def some(i, _):
            take_rows(i * UNROLL, UNROLL, t + 1, later)
            return 0

        lax.fori_loop(0, H // UNROLL, some, 0)

    flat = jnp.transpose(reply_s[...])
    flat = (flat[:G] + flat[G:]) * (1.0 / river_total)
    owners = out_ref.shape[0]
    each = G // owners
    blocks = HP // 128
    for turn in range(turns):

        @pl.when(t == turn)
        def _():
            for j in range(blocks):
                piece = flat[:, j * 128 : (j + 1) * 128].reshape(owners, each, 128)
                row = (turn * blocks + j) * each
                out_ref[:, row : row + each, :] = piece


def shifted(x, axis, shift):
    return lax.ppermute(x, axis, [(i, (i + shift) % 4) for i in range(4)])


def per_device(
    river_regret,
    turn_regret,
    river_bucket,
    turn_bucket,
    ranks,
    turn_card,
    river_card,
    player_range,
    opp_range,
    call_prob,
    base_pot,
):
    turns, rivers, _ = river_bucket.shape
    boards = turns * rivers
    devices = 128
    owners = 16
    each = G // owners
    river_total = rivers * owners
    owned, towned = river_regret.shape[0], turn_regret.shape[0]
    buckets, tbuckets = owned * devices, towned * devices
    disjoint, holds, out_of, rperm, tperm, cards = constants()
    params = pltpu.CompilerParams(vmem_limit_bytes=VMEM_LIMIT)
    pot = base_pot.reshape(1, G)
    calls = jnp.transpose(call_prob, (0, 3, 1, 2))
    river_at_turn = river_card.T
    rest = owned + towned
    swap = [(0, 1), (1, 0)]
    turn_row = turns * (HP // 128) * each
    river_row = turn_row + towned // 2
    sent_rows = river_row + owned

    with jax.named_scope("strategies"):
        strategies, *indices = pl.pallas_call(
            strategy_kernel,
            out_shape=[
                jax.ShapeDtypeStruct((owners, rest, C), F32),
                jax.ShapeDtypeStruct((boards, INDEX_ROW // 128, 128), jnp.int32),
                jax.ShapeDtypeStruct((boards, INDEX_ROW // 128, 128), jnp.int32),
                jax.ShapeDtypeStruct((turns, INDEX_ROW // 128, 128), jnp.int32),
            ],
            compiler_params=params,
            name="strategies",
        )(river_regret, turn_regret, rperm, tperm, river_bucket, turn_bucket)
        index, river_at, turn_at = (a.reshape(-1) for a in indices)
        plane = lax.all_to_all(strategies, ("z", "y"), 0, 0).reshape(-1, C)

    def whole(shape):
        return pl.BlockSpec(shape, lambda i, *_: (0,) * len(shape))

    def per_turn(shape, count=1):
        return pl.BlockSpec((count,) + shape, lambda i, *_: (i,) + (0,) * len(shape))

    def per_board(shape):
        return per_turn(shape, rivers)

    def payoffs(start, count, known=()):
        def of_turn(shape, each_turn=1):
            return pl.BlockSpec(
                (each_turn,) + shape, lambda i, *_: (i + start,) + (0,) * len(shape)
            )

        return pl.pallas_call(
            functools.partial(payoff_kernel, rivers, start),
            grid_spec=pltpu.PrefetchScalarGridSpec(
                num_scalar_prefetch=2,
                grid=(count,),
                in_specs=[
                    of_turn((rivers, H)),
                    of_turn((H, rivers, C)),
                    whole((G, H)),
                    whole((1, G)),
                    whole((HP, HP)),
                    whole((64, HP)),
                    whole((HP, 256)),
                    whole((C, C)),
                    whole((8, HP)),
                ]
                + [pl.BlockSpec(memory_space=pl.ANY)] * len(known),
                out_specs=[of_turn((HP, C), rivers), of_turn((HP, C))],
                scratch_shapes=[
                    pltpu.VMEM((8, HP), jnp.int32),
                    pltpu.VMEM((rivers * HP, C), F32),
                    pltpu.VMEM((C, HP), F32),
                    pltpu.VMEM((HP, C), F32),
                    pltpu.VMEM((rivers, HP, 2 * C), BF),
                ],
            ),
            out_shape=[
                jax.ShapeDtypeStruct((boards, HP, C), F32),
                jax.ShapeDtypeStruct((turns, HP, C), F32),
            ],
            input_output_aliases={11 + i: i for i in range(len(known))},
            compiler_params=params,
            cost_estimate=pl.CostEstimate(
                flops=count * 8 * 10**9, bytes_accessed=10**6, transcendentals=0
            ),
            name="payoffs",
        )(
            turn_card,
            river_at_turn,
            ranks,
            calls,
            opp_range,
            pot,
            disjoint,
            holds,
            out_of,
            tperm,
            cards,
            *known,
        )

    with jax.named_scope("payoffs"):
        delta, bet = payoffs(0, turns)
    with jax.named_scope("strategies"):
        plane, delta = lax.optimization_barrier((plane, delta))
        onward = [(2 * i, (2 * i + 2) % 8) for i in range(4)]
        onward += [(2 * i + 1, (2 * i + 7) % 8) for i in range(4)]
        back = [(j, i) for i, j in onward]
        near = lax.ppermute(plane, ("x", "core"), onward)
        last = lax.ppermute(plane, ("x", "core"), back)

    with jax.named_scope("river_sums"):
        mine, theirs = pl.pallas_call(
            sum_kernel,
            grid_spec=pltpu.PrefetchScalarGridSpec(
                num_scalar_prefetch=1,
                grid=(boards,),
                in_specs=[per_turn((HP, C))],
                out_specs=[whole((4, owners * owned, C))] * 2,
                scratch_shapes=[pltpu.VMEM((buckets, C), F32)] * TABLES,
            ),
            out_shape=[jax.ShapeDtypeStruct((4, owners * owned, C), F32)] * 2,
            compiler_params=params,
            cost_estimate=pl.CostEstimate(
                flops=22 * 10**9, bytes_accessed=10**6, transcendentals=0
            ),
            name="sums",
        )(index, delta)
        near, last, theirs = lax.optimization_barrier((near, last, theirs))
        got = lax.ppermute(theirs, "core", swap)
        far = lax.ppermute(near, ("x", "core"), onward)
        chip = mine + got
        chip, far = lax.optimization_barrier((chip, far))
        columns = lax.all_to_all(chip, "x", 0, 0)
        own = [plane, near, far, last]
        pieces = own + [lax.ppermute(piece, "core", swap) for piece in own]
        delta, chip, *pieces = lax.optimization_barrier((delta, chip, *pieces))

    with jax.named_scope("replies"):
        replies, held, lent = pl.pallas_call(
            functools.partial(reply_kernel, turns, rivers, river_total, len(pieces)),
            grid_spec=pltpu.PrefetchScalarGridSpec(
                num_scalar_prefetch=4,
                grid=(turns,),
                in_specs=[
                    per_turn((rivers, H)),
                    whole((turns, H)),
                    per_board((HP, C)),
                    per_turn((HP, C)),
                    whole((G, H)),
                    whole((1, G)),
                    whole((HP, HP)),
                    whole((64, HP)),
                    whole((HP, 256)),
                    whole((8, HP)),
                ]
                + [pl.BlockSpec(memory_space=pl.ANY)] * len(pieces),
                out_specs=[
                    whole((owners, sent_rows, 128)),
                    whole((4, owners * towned // 2, C)),
                    whole((4, owners * towned // 2, C)),
                ],
                scratch_shapes=[
                    pltpu.VMEM((tbuckets // 2, C), F32),
                    pltpu.VMEM((rest * devices, C), F32),
                    pltpu.VMEM((2, rivers + 1, HP, C), F32),
                    pltpu.VMEM((HP, C), F32),
                    pltpu.VMEM((C, HP), F32),
                    pltpu.VMEM((8, HP), jnp.int32),
                    pltpu.VMEM((8, HP), jnp.int32),
                    pltpu.VMEM((rivers, HP, C), F32),
                    pltpu.VMEM((rivers, HP, 2 * C), BF),
                    pltpu.VMEM((rivers, 256, C), BF),
                    pltpu.VMEM((HP, C), F32),
                    pltpu.SemaphoreType.DMA((len(pieces),)),
                ],
            ),
            out_shape=[
                jax.ShapeDtypeStruct((owners, sent_rows, 128), F32),
                jax.ShapeDtypeStruct((4, owners * towned // 2, C), F32),
                jax.ShapeDtypeStruct((4, owners * towned // 2, C), F32),
            ],
            compiler_params=params,
            cost_estimate=pl.CostEstimate(
                flops=30 * 10**9, bytes_accessed=10**6, transcendentals=0
            ),
            name="replies",
        )(
            river_at,
            turn_at,
            turn_card,
            river_at_turn,
            ranks,
            turn_bucket,
            delta,
            bet,
            player_range,
            pot,
            disjoint,
            holds,
            out_of,
            cards,
            *pieces,
        )
    with jax.named_scope("turn_sums"):
        held = held + lax.ppermute(lent, "core", swap)
        turn_parts = [held[0]] + [shifted(held[s], "x", s) for s in (2, 1, 3)]

    with jax.named_scope("exchange"):
        replies, columns, turn_parts = lax.optimization_barrier((replies, columns, turn_parts))
        turn_sums, column = sum(turn_parts[1:], turn_parts[0]), columns.sum(0)
        sent = replies.at[:, turn_row:river_row].set(turn_sums.reshape(owners, -1, 128))
        sent = sent.at[:, river_row:].set(column.reshape(owners, -1, 128))
        came = lax.all_to_all(sent, ("z", "y"), 0, 0)

    with jax.named_scope("update"):
        new_river, new_turn, br_value = pl.pallas_call(
            functools.partial(update_kernel, 1.0 / river_total, each),
            out_shape=[
                jax.ShapeDtypeStruct(river_regret.shape, F32),
                jax.ShapeDtypeStruct(turn_regret.shape, F32),
                jax.ShapeDtypeStruct((turns, each, H), F32),
            ],
            compiler_params=params,
            name="update",
        )(came, river_regret, turn_regret, rperm, tperm)
    return new_river, new_turn, br_value


def solution(mesh):
    mesh = Mesh(mesh.devices.reshape(4, 2, 4, 4), AXES)
    turn, river = AXES[:2], AXES[2:]
    placed = (
        P(AXES, None),
        P(AXES, None),
        P(turn, river, None),
        P(turn, None),
        P(turn, river, None),
        P(turn),
        P(turn, river),
        P(),
        P(),
        P(turn, river, None, None),
        P(),
    )
    return jax.shard_map(
        per_device,
        mesh=mesh,
        in_specs=placed,
        out_specs=(P(AXES, None), P(AXES, None), P(turn, river, None)),
        check_vma=False,
    )
```
